512 devices in a mesh: rows: 64 (over x, y, core), cols: 8 (over z).
Axes of the slice: x: 4, y: 8, z: 8, core: 2. Of those that a mesh axis runs over, the one named last changes fastest.
Arguments:
- data: float32 [80, 32768], P(None, 'rows'), may hold values from -6 to 6
- source: int32 [32768], P('rows'), may hold values from 0 to 32767, as said below
- near_tiles: bfloat16 [1920, 1024, 512], P('rows', 'cols'), may hold values from -0.046875 to 0.046875
- near_rows: int32 [1920, 8], P('rows', 'cols'), may hold values from 0 to 3, as said below
- near_cols: int32 [1920, 8], P('rows', 'cols'), may hold values from 0 to 9, as said below
- near_count: int32 [64, 8], P('rows', 'cols'), may hold values from 0 to 30, as said below
- far_left: bfloat16 [192, 32768], P('cols', 'rows'), may hold values from -0.4375 to 0.4375
- far_right: bfloat16 [1536, 40960], P('rows', 'cols'), may hold values from -0.078125 to 0.078125
Outputs:
- slip: float32 [80, 40960], P(None, ('cols', 'rows'))
- misfit: float32 [80, 32768], P(None, 'rows')
The draws below stay inside these ranges and needn't reach their ends.
Inputs may be any that keep to these rules, and one draw needn't show every extreme that they name: source is a permutation of the pixels; the burst position source[j] lies in the cluster of pixel j or in one of the two clusters beside it, counted cyclically. The slots of one cluster pair name distinct pairs of sub-clusters (near_rows, near_cols). `near_cols`: see near_rows. Slots at or beyond near_count are ignored; near_count[r, c] is zero unless c is the patch cluster adjacent to pixel cluster r (r times the number of patch clusters over the number of pixel clusters, rounded down) or the next one after it, counted cyclically; there it is 7 or more.
All inputs are finite; a program needn't handle non-finite values.
Results may differ from the reference program's by a relative error of at most 0.02.
Values may be sent and summed in bfloat16 or wider, within the bound.
A program may use at most 64 MiB of HBM per device.

```python
import jax
import jax.numpy as jnp
from jax import lax

P_DEV = 512
Q_DEV = 5120
RANK = 24
BP = 128
BQ = 512
NT = 30
REALIZATIONS = 80
ITERS = 2
PIXELS = 32768
SLIP = 40960
N_ROWS = 64
N_COLS = 8


def pair_blocks(key):
    key = jax.random.fold_in(key, 77)
    sub_total = P_DEV // BP * (Q_DEV // BQ)
    pair_keys = jax.random.split(key, N_ROWS * N_COLS)
    chosen = jax.vmap(lambda single: jax.random.permutation(single, sub_total)[:NT])(pair_keys)
    chosen = chosen.reshape(N_ROWS, N_COLS, NT).transpose(0, 2, 1).reshape(N_ROWS * NT, N_COLS)
    return chosen.astype(jnp.int32)


def draw_near_rows(key, part):
    chosen = pair_blocks(key)
    return (chosen // (Q_DEV // BQ)).astype(jnp.int32)


def draw_near_cols(key, part):
    chosen = pair_blocks(key)
    return (chosen % (Q_DEV // BQ)).astype(jnp.int32)


def draw_near_count(key, part):
    key = jax.random.fold_in(key, 3)
    first_key, second_key = jax.random.split(key)
    level = jax.random.randint(first_key, (N_ROWS, N_COLS), 0, 17).astype(jnp.int32)
    counts = NT // 4 + (NT - NT // 4) * level * level // 256
    row_ids = jnp.arange(N_ROWS, dtype=jnp.int32)[:, None]
    col_ids = jnp.arange(N_COLS, dtype=jnp.int32)[None, :]
    home = row_ids * N_COLS // N_ROWS
    after = (home + 1) % N_COLS
    adjacent = jnp.logical_or(col_ids == home, col_ids == after)
    heavy_row = jax.random.randint(second_key, (), 0, N_ROWS).astype(jnp.int32)
    heavy = jnp.logical_and(row_ids == heavy_row, col_ids == home)
    counts = jnp.where(adjacent, counts, 0)
    return jnp.where(heavy, NT, counts).astype(jnp.int32)


def block_shuffle(key):
    block_keys = jax.random.split(key, N_ROWS)
    inside = jax.vmap(lambda single: jax.random.permutation(single, P_DEV))(block_keys)
    offsets = (jnp.arange(N_ROWS, dtype=jnp.int32) * P_DEV)[:, None]
    return (inside.astype(jnp.int32) + offsets).reshape(PIXELS)


def draw_source(key, part):
    key = jax.random.fold_in(key, 4)
    keys_list = jax.random.split(key, 5)
    first_mix = block_shuffle(keys_list[0])
    middle_mix = block_shuffle(keys_list[1])
    last_mix = block_shuffle(keys_list[2])
    forward_step = jax.random.randint(keys_list[3], (), P_DEV // 4, P_DEV // 2 + 1).astype(jnp.int32)
    backward_step = jax.random.randint(keys_list[4], (), P_DEV // 4, P_DEV // 2 + 1).astype(jnp.int32)
    moved = (first_mix + forward_step) % PIXELS
    moved = jnp.take(middle_mix, moved)
    moved = (moved - backward_step + PIXELS) % PIXELS
    return jnp.take(last_mix, moved).astype(jnp.int32)


def steps_of(key, extent, cuts, smallest, top_value):
    level, own = 1.0, jax.random.fold_in(key, 6)
    for position, shards_of in cuts:
        draws = jnp.exp(jax.random.uniform(jax.random.fold_in(own, position), (shards_of,), jnp.float32, smallest / len(cuts), top_value / len(cuts)))
        level = level * jnp.repeat(draws, extent[position] // shards_of).reshape([-1 if axis == position else 1 for axis in range(len(extent))])
    return level


def bell_draw(stream_key, shape, width, bound, cuts=(), kind=jnp.bfloat16):
    entries = jax.random.normal(stream_key, shape, jnp.float32) * width
    if len(cuts) > 0:
        entries = steps_of(stream_key, shape, cuts, -0.22, 0.18) * entries
    return jnp.clip(entries, min=-bound, max=bound).astype(kind)


def setup_inputs(seed: int = 0) -> dict:
    seeds = jax.random.split(jax.random.key(seed), 9)
    return {
        "data": bell_draw(seeds[0], (REALIZATIONS, PIXELS), 1.0, 6.0, ((1, 64),), jnp.float32),
        "source": draw_source(jax.random.fold_in(seeds[8], 71), 0),
        "near_tiles": bell_draw(seeds[2], (N_ROWS * NT, N_COLS * BP, BQ), (BQ * NT) ** -0.5, 0.046875, ((0, 64), (1, 8))),
        "near_rows": draw_near_rows(jax.random.fold_in(seeds[8], 71), 0),
        "near_cols": draw_near_cols(jax.random.fold_in(seeds[8], 71), 0),
        "near_count": draw_near_count(jax.random.fold_in(seeds[8], 71), 0),
        "far_left": bell_draw(seeds[6], (N_COLS * RANK, PIXELS), (RANK * N_COLS) ** -0.5, 0.4375, ((0, 8), (1, 64))),
        "far_right": bell_draw(seeds[7], (N_ROWS * RANK, SLIP), Q_DEV ** -0.5, 0.078125, ((0, 64), (1, 8))),
    }


EPSILON = 1e-06

def block_forward(vector_b, tiles, rows_index, cols_index, count, left_factor, right_factor):
    inner = jnp.dot(vector_b, right_factor.T, preferred_element_type=jnp.float32).astype(jnp.bfloat16)
    far_term = jnp.dot(inner, left_factor, preferred_element_type=jnp.float32)
    pieces = jnp.take(vector_b.reshape(REALIZATIONS, Q_DEV // BQ, BQ), cols_index, axis=1)
    products = jnp.einsum('knq,npq->nkp', pieces.astype(jnp.float32), tiles.astype(jnp.float32))
    live = (jnp.arange(NT) < count).astype(jnp.float32)
    placing = (rows_index[:, None] == jnp.arange(P_DEV // BP)[None, :]).astype(jnp.float32) * live[:, None]
    near_term = jnp.einsum('nkp,na->kap', products, placing).reshape(REALIZATIONS, P_DEV)
    return far_term + near_term

def block_adjoint(pixel_b, tiles, rows_index, cols_index, count, left_factor, right_factor):
    outer = jnp.dot(pixel_b, left_factor.T, preferred_element_type=jnp.float32).astype(jnp.bfloat16)
    far_term = jnp.dot(outer, right_factor, preferred_element_type=jnp.float32)
    pieces = jnp.take(pixel_b.reshape(REALIZATIONS, P_DEV // BP, BP), rows_index, axis=1)
    products = jnp.einsum('knp,npq->nkq', pieces.astype(jnp.float32), tiles.astype(jnp.float32))
    live = (jnp.arange(NT) < count).astype(jnp.float32)
    placing = (cols_index[:, None] == jnp.arange(Q_DEV // BQ)[None, :]).astype(jnp.float32) * live[:, None]
    near_term = jnp.einsum('nkq,nb->kbq', products, placing).reshape(REALIZATIONS, Q_DEV)
    return far_term + near_term

def grouped(near_tiles, near_rows, near_cols, far_left, far_right):
    tiles_grid = near_tiles.reshape(N_ROWS, NT, N_COLS, BP, BQ)
    rows_grid = near_rows.reshape(N_ROWS, NT, N_COLS)
    cols_grid = near_cols.reshape(N_ROWS, NT, N_COLS)
    left_grid = far_left.reshape(N_COLS, RANK, N_ROWS, P_DEV)
    right_grid = far_right.reshape(N_ROWS, RANK, N_COLS, Q_DEV)
    return (tiles_grid, rows_grid, cols_grid, left_grid, right_grid)

def forward_all(vector_b, grids, near_count):
    tiles_grid, rows_grid, cols_grid, left_grid, right_grid = grids
    vector_cols = vector_b.reshape(REALIZATIONS, N_COLS, Q_DEV)

    def one_row(index):
        per_col = jax.vmap(block_forward, in_axes=(1, 1, 1, 1, 0, 0, 1))(vector_cols, tiles_grid[index], rows_grid[index], cols_grid[index], near_count[index], left_grid[:, :, index, :], right_grid[index])
        return lax.optimization_barrier(jnp.sum(per_col, axis=0))
    rows_out = lax.map(one_row, jnp.arange(N_ROWS, dtype=jnp.int32))
    return rows_out.transpose(1, 0, 2).reshape(REALIZATIONS, PIXELS)

def adjoint_all(pixel_b, grids, near_count):
    tiles_grid, rows_grid, cols_grid, left_grid, right_grid = grids
    pixel_rows = pixel_b.reshape(REALIZATIONS, N_ROWS, P_DEV)

    def add_row(total, index):
        part = jax.vmap(block_adjoint, in_axes=(None, 1, 1, 1, 0, 0, 1))(pixel_rows[:, index, :], tiles_grid[index], rows_grid[index], cols_grid[index], near_count[index], left_grid[:, :, index, :], right_grid[index])
        return (total + part, None)
    start = jnp.zeros((N_COLS, REALIZATIONS, Q_DEV), jnp.float32)
    total, _ = lax.scan(add_row, start, jnp.arange(N_ROWS, dtype=jnp.int32))
    return total.transpose(1, 0, 2).reshape(REALIZATIONS, SLIP)

def norm_of(field):
    return jnp.sqrt(lax.optimization_barrier(jnp.sum(field * field, axis=1)) + EPSILON)

def reference(data, source, near_tiles, near_rows, near_cols, near_count, far_left, far_right):
    grids = grouped(near_tiles, near_rows, near_cols, far_left, far_right)
    observed = jnp.take(data, source, axis=1)
    beta = norm_of(observed)
    left = observed / beta[:, None]
    right_raw = adjoint_all(left.astype(jnp.bfloat16), grids, near_count)
    alpha = norm_of(right_raw)
    right = right_raw / alpha[:, None]
    direction = right
    solution = jnp.zeros_like(right)
    phibar = beta
    rhobar = alpha
    for step in range(ITERS):
        left = forward_all(right.astype(jnp.bfloat16), grids, near_count) - alpha[:, None] * left
        beta = norm_of(left)
        left = left / beta[:, None]
        rho = jnp.sqrt(rhobar * rhobar + beta * beta)
        cosine = rhobar / rho
        sine = beta / rho
        phi = cosine * phibar
        phibar = sine * phibar
        solution = solution + (phi / rho)[:, None] * direction
        if step + 1 < ITERS:
            right_raw = adjoint_all(left.astype(jnp.bfloat16), grids, near_count) - beta[:, None] * right
            alpha = norm_of(right_raw)
            right = right_raw / alpha[:, None]
            theta = sine * alpha
            rhobar = -cosine * alpha
            direction = right - (theta / rho)[:, None] * direction
    misfit = observed - forward_all(solution.astype(jnp.bfloat16), grids, near_count)
    return (solution, misfit)
```

```python
import functools

import jax
import jax.numpy as jnp
from jax import lax
from jax.experimental import pallas as pl
from jax.experimental.pallas import tpu as pltpu
from jax.sharding import PartitionSpec as P

EPSILON = 1e-06
LANE = 128
TILE = 16
MESH = pl.DeviceIdType.MESH
F32 = jnp.float32
BF16 = jnp.bfloat16

SCRATCH = (
    "tiles", "halo", "onehot", "g", "pc_send", "pc_recv", "px_send", "px_recv", "q_send", "q_recv", "v",
    "f_send", "f_recv", "f_all", "w1", "coef", "sa_send", "sa_recv", "sb_send", "sb_recv", "sz_send", "sz_recv",
    "tile_sem", "halo_ss", "halo_rs", "c_ss", "c_rs", "x_ss", "x_rs", "y_ss", "y_rs", "yg_ss", "yg_rs",
    "xg_ss", "xg_rs", "cg_ss", "cg_rs", "z_ss", "z_rs", "zg_ss", "zg_rs", "sa_ss", "sa_rs", "sb_ss", "sb_rs",
    "sz_ss", "sz_rs",
)


class Sizes:
    def __init__(self, dims, nz, realiz, pixels, width, slots, rank, tile_rows, tile_cols):
        self.nx, self.ny, self.cores = dims
        self.nz = nz
        self.rows = self.nx * self.ny * self.cores
        self.nq = self.nx * self.cores
        self.realiz, self.pixels, self.width = realiz, pixels, width
        self.slots, self.rank, self.tile_rows, self.tile_cols = slots, rank, tile_rows, tile_cols
        self.groups = realiz // TILE
        self.chunk = width // self.nq
        self.nb = self.chunk // LANE
        self.tb = self.nb * self.groups
        self.tp = -(-self.tb // self.ny)
        self.tq = self.tp * self.ny
        self.fb = pixels // LANE
        self.ft = self.fb * self.groups
        self.zp = -(-self.ft // nz)
        self.fz = self.zp * nz


def scratch_shapes(s):
    dma = pltpu.SemaphoreType.DMA
    return [
        pltpu.VMEM((s.slots, s.tile_rows, s.tile_cols), BF16),
        pltpu.VMEM((2, s.realiz, s.pixels), F32),
        pltpu.VMEM((3, s.pixels, s.pixels), BF16),
        pltpu.VMEM((s.nq, s.pixels, s.chunk), BF16),
        pltpu.VMEM((2, s.nx, s.tb, TILE, LANE), BF16),
        pltpu.VMEM((2, s.nx, s.tb, TILE, LANE), BF16),
        pltpu.VMEM((2, s.nx - 1, s.tb, TILE, LANE), BF16),
        pltpu.VMEM((2, s.nx - 1, s.tb, TILE, LANE), BF16),
        pltpu.VMEM((2, s.tq, TILE, LANE), BF16),
        pltpu.VMEM((2, s.ny - 1, s.tp, TILE, LANE), BF16),
        pltpu.VMEM((2, s.nq, s.tq, TILE, LANE), BF16),
        pltpu.VMEM((2, s.fz, TILE, LANE), BF16),
        pltpu.VMEM((2, s.nz - 1, s.zp, TILE, LANE), BF16),
        pltpu.VMEM((2, s.fz, TILE, LANE), BF16),
        pltpu.VMEM((s.tp, TILE, LANE), F32),
        pltpu.VMEM((2, s.groups, TILE, LANE), F32),
        pltpu.VMEM((3, 8, LANE), F32),
        pltpu.VMEM((3, s.nq - 1, 8, LANE), F32),
        pltpu.VMEM((3, 8, LANE), F32),
        pltpu.VMEM((3, s.ny - 1, 8, LANE), F32),
        pltpu.VMEM((2, 8, LANE), F32),
        pltpu.VMEM((2, s.nz - 1, 8, LANE), F32),
        dma((1,)),
        dma((1,)),
        dma((2,)),
        dma((2,)),
        dma((2, s.nx)),
        dma((2,)),
        dma((2, s.nx)),
        dma((2,)),
        dma((2,)),
        dma((2,)),
        dma((2,)),
        dma((2,)),
        dma((2, s.nx)),
        dma((2,)),
        dma((2, s.nx)),
        dma((2,)),
        dma((2,)),
        dma((2,)),
        dma((2,)),
        dma((3,)),
        dma((3,)),
        dma((3,)),
        dma((3,)),
        dma((2,)),
        dma((2,)),
    ]


def far_first(count):
    return sorted(range(1, count), key=lambda d: (-min(d, count - d), d))


def near_first(count):
    return sorted(range(1, count), key=lambda d: (min(d, count - d), d))


def await_bytes(ref, sem):
    pltpu.make_async_copy(ref, ref, sem).wait()


def to_row(column):
    rows = column.shape[0]
    wide = jnp.broadcast_to(column, (rows, LANE))
    wide = jnp.concatenate([wide, jnp.zeros((LANE - rows, LANE), F32)], axis=0)
    return wide.T[0:8]


def from_row(row, rows):
    return jnp.broadcast_to(row[0:1], (LANE, LANE)).T[0:rows]


def row_sums(blocks):
    total = blocks[0] * blocks[0]
    for block in blocks[1:]:
        total = total + block * block
    return jnp.sum(total, axis=1, keepdims=True)


def lane_blocks(value):
    return [value[:, j * LANE : (j + 1) * LANE] for j in range(value.shape[1] // LANE)]


def as_tiles(value):
    groups = value.shape[0] // TILE
    return jnp.concatenate([b.reshape(groups, TILE, LANE) for b in lane_blocks(value)], axis=0)


def from_tiles(tiles, groups):
    count = tiles.shape[0] // groups
    return jnp.concatenate(
        [tiles[j * groups : (j + 1) * groups].reshape(groups * TILE, LANE) for j in range(count)], axis=1
    )


def three_parts(value):
    high = value.astype(BF16)
    rest = value - high.astype(F32)
    middle = rest.astype(BF16)
    low = (rest - middle.astype(F32)).astype(BF16)
    return jnp.concatenate([high, middle, low], axis=0)


def kernel(s, data, source, slot_of, live, tiles_hbm, far_left, far_right, slip, misfit, *scratch):
    m = dict(zip(SCRATCH, scratch, strict=True))
    place = lax.axis_index("rows")
    z = lax.axis_index("cols")
    core = lax.rem(place, 2)
    chip = place // 2
    y = lax.rem(chip, s.ny)
    x = chip // s.ny
    other = 1 - core
    own_q = core * s.nx + x

    def at(xx, yy, cc):
        return ((xx * s.ny + yy) * 2 + cc, z)

    def cross(d):
        q = lax.rem(own_q + d, s.nq)
        return at(lax.rem(q, s.nx), y, q // s.nx)

    def along_y(d):
        return at(x, lax.rem(y + d, s.ny), core)

    def along_z(d):
        return (place, lax.rem(z + d, s.nz))

    mate = at(x, y, other)

    def send(src, dst, send_sem, recv_sem, device):
        pltpu.make_async_remote_copy(
            src_ref=src, dst_ref=dst, send_sem=send_sem, recv_sem=recv_sem, device_id=device, device_id_type=MESH
        ).start()

    tile_copy = pltpu.make_async_copy(tiles_hbm, m["tiles"], m["tile_sem"].at[0])
    tile_copy.start()

    step_out = lax.rem(place + s.rows + 2 * core - 1, s.rows)
    partners = [cross(d) for d in range(1, s.nq)]
    partners += [along_y(d) for d in range(1, s.ny)]
    partners += [along_z(d) for d in range(1, s.nz)]
    partners += [(step_out, z)]
    barrier = pltpu.get_barrier_semaphore()
    for device in partners:
        pl.semaphore_signal(barrier, inc=1, device_id=device, device_id_type=MESH)
    pl.semaphore_wait(barrier, len(partners))

    after = lax.rem(place + 1, s.rows)
    before = lax.rem(place + s.rows - 1, s.rows)
    send(data, m["halo"].at[0], m["halo_ss"].at[0], m["halo_rs"].at[0], (after, z))
    send(data, m["halo"].at[1], m["halo_ss"].at[0], m["halo_rs"].at[1], (before, z))

    total = s.rows * s.pixels
    offset = source[...] + s.pixels - place * s.pixels
    offset = jnp.where(offset < 0, offset + total, offset)
    offset = jnp.where(offset >= total, offset - total, offset)
    index = lax.broadcasted_iota(jnp.int32, (s.pixels, s.pixels), 0)
    for k in range(3):
        m["onehot"][k] = jnp.where(index == offset - k * s.pixels, 1.0, 0.0).astype(BF16)

    tile_copy.wait()
    per_row = s.width // s.tile_cols
    half = per_row // 2
    half_blocks = half * s.tile_cols // LANE
    bands = s.pixels // s.tile_rows

    def build(i, carry):
        g, a = i // bands, lax.rem(i, bands)
        pixel = pl.ds(pl.multiple_of(a * s.tile_rows, s.tile_rows), s.tile_rows)
        lefts = far_left[:, pixel]
        for b in range(half):
            where = a * per_row + g * half + b
            column = pl.ds(pl.multiple_of((g * half + b) * s.tile_cols, s.tile_cols), s.tile_cols)
            block = lax.dot_general(lefts, far_right[:, column], (((0,), (0,)), ((), ())), preferred_element_type=F32)
            block = block + m["tiles"][slot_of[where]].astype(F32) * live[where]
            block = block.astype(BF16)
            for k in range(s.tile_cols // LANE):
                j = b * (s.tile_cols // LANE) + k
                q = g * (half_blocks // s.nb) + j // s.nb
                lane = (j % s.nb) * LANE
                m["g"][q, pixel, lane : lane + LANE] = block[:, k * LANE : (k + 1) * LANE]
        return carry

    lax.fori_loop(0, 2 * bands, build, 0)

    seen = jnp.dot(three_parts(data[...]), m["onehot"][1], preferred_element_type=F32)
    for k in range(2):
        await_bytes(m["halo"].at[k], m["halo_rs"].at[k])
        seen = seen + jnp.dot(three_parts(m["halo"][k]), m["onehot"][2 * k], preferred_element_type=F32)
    n = s.realiz
    observed = (seen[0:n] + seen[n : 2 * n]) + seen[2 * n : 3 * n]
    misfit[...] = observed

    def sum_start(i, column):
        m["sa_send"][i] = to_row(column)
        for d in range(1, s.nq):
            send(m["sa_send"].at[i], m["sa_recv"].at[i, d - 1], m["sa_ss"].at[i], m["sa_rs"].at[i], cross(d))

    def sum_middle(i):
        await_bytes(m["sa_recv"].at[i], m["sa_rs"].at[i])
        m["sb_send"][i] = m["sa_send"][i] + jnp.sum(m["sa_recv"][i], axis=0)
        for d in range(1, s.ny):
            send(m["sb_send"].at[i], m["sb_recv"].at[i, d - 1], m["sb_ss"].at[i], m["sb_rs"].at[i], along_y(d))

    def sum_end(i):
        await_bytes(m["sb_recv"].at[i], m["sb_rs"].at[i])
        return from_row(m["sb_send"][i] + jnp.sum(m["sb_recv"][i], axis=0), n)

    def adjoint(it, pixel_b):
        def part(q):
            return as_tiles(jnp.dot(pixel_b, m["g"][q], preferred_element_type=F32))

        order = far_first(s.nx) + [0]
        for d in order:
            m["pc_send"][it, d] = part(other * s.nx + lax.rem(x + d, s.nx)).astype(BF16)
            send(m["pc_send"].at[it, d], m["pc_recv"].at[it, d], m["c_ss"].at[it], m["c_rs"].at[it, d], mate)
        own = None
        for d in order:
            xx = lax.rem(x + d, s.nx)
            own = part(core * s.nx + xx)
            await_bytes(m["pc_recv"].at[it, d], m["c_rs"].at[it, d])
            own = own + m["pc_recv"][it, d].astype(F32)
            if d > 0:
                m["px_send"][it, d - 1] = own.astype(BF16)
                send(
                    m["px_send"].at[it, d - 1],
                    m["px_recv"].at[it, d - 1],
                    m["x_ss"].at[it],
                    m["x_rs"].at[it, d - 1],
                    at(xx, y, core),
                )
        sum_middle(it)
        for d in near_first(s.nx):
            await_bytes(m["px_recv"].at[it, d - 1], m["x_rs"].at[it, d - 1])
            own = own + m["px_recv"][it, d - 1].astype(F32)
        m["q_send"][it, 0 : s.tb] = own.astype(BF16)
        if s.tq > s.tb:
            m["q_send"][it, s.tb : s.tq] = jnp.zeros((s.tq - s.tb, TILE, LANE), BF16)
        for d in far_first(s.ny):
            piece = pl.ds(lax.rem(y + d, s.ny) * s.tp, s.tp)
            send(
                m["q_send"].at[it, piece],
                m["q_recv"].at[it, d - 1],
                m["y_ss"].at[it],
                m["y_rs"].at[it],
                along_y(d),
            )
        await_bytes(m["q_recv"].at[it], m["y_rs"].at[it])
        share = m["q_send"][it, pl.ds(y * s.tp, s.tp)].astype(F32)
        for d in range(s.ny - 1):
            share = share + m["q_recv"][it, d].astype(F32)
        return share

    def forward(it, share):
        v = m["v"]
        mine = v.at[it, own_q, pl.ds(y * s.tp, s.tp)]
        mine[...] = share.astype(BF16)
        for d in far_first(s.ny):
            send(mine, mine, m["yg_ss"].at[it], m["yg_rs"].at[it], along_y(d))
        await_bytes(m["q_recv"].at[it], m["yg_rs"].at[it])
        ready = v.at[it, own_q, 0 : s.tb]
        for d in far_first(s.nx):
            send(ready, ready, m["xg_ss"].at[it], m["xg_rs"].at[it, d - 1], at(lax.rem(x + d, s.nx), y, core))
        send(ready, ready, m["cg_ss"].at[it], m["cg_rs"].at[it, 0], mate)

        def part(q):
            return lax.dot_general(
                from_tiles(v[it, q, 0 : s.tb], s.groups),
                m["g"][q],
                (((1,), (1,)), ((), ())),
                preferred_element_type=F32,
            )

        total = part(own_q)
        for d in near_first(s.nx):
            q = core * s.nx + lax.rem(x + s.nx - d, s.nx)
            came = v.at[it, q, 0 : s.tb]
            await_bytes(came, m["xg_rs"].at[it, d - 1])
            send(came, came, m["cg_ss"].at[it], m["cg_rs"].at[it, d], mate)
            total = total + part(q)
        for d in [0] + near_first(s.nx):
            q = other * s.nx + lax.rem(x + s.nx - d, s.nx)
            await_bytes(v.at[it, q, 0 : s.tb], m["cg_rs"].at[it, d])
            total = total + part(q)

        m["f_send"][it, 0 : s.ft] = as_tiles(total).astype(BF16)
        if s.fz > s.ft:
            m["f_send"][it, s.ft : s.fz] = jnp.zeros((s.fz - s.ft, TILE, LANE), BF16)
        for d in far_first(s.nz):
            piece = pl.ds(lax.rem(z + d, s.nz) * s.zp, s.zp)
            send(
                m["f_send"].at[it, piece],
                m["f_recv"].at[it, d - 1],
                m["z_ss"].at[it],
                m["z_rs"].at[it],
                along_z(d),
            )

        def squares(q, running):
            for j in range(s.nb):
                block = v[it, q, j * s.groups : (j + 1) * s.groups].astype(F32).reshape(n, LANE)
                running = running + block * block
            return running

        running = lax.fori_loop(0, s.nq, squares, jnp.zeros((n, LANE), F32))
        m["sz_send"][it] = to_row(jnp.sum(running, axis=1, keepdims=True))
        for d in far_first(s.nz):
            send(m["sz_send"].at[it], m["sz_recv"].at[it, d - 1], m["sz_ss"].at[it], m["sz_rs"].at[it], along_z(d))

        await_bytes(m["f_recv"].at[it], m["z_rs"].at[it])
        reduced = m["f_send"][it, pl.ds(z * s.zp, s.zp)].astype(F32)
        for d in range(s.nz - 1):
            reduced = reduced + m["f_recv"][it, d].astype(F32)
        mine = m["f_all"].at[it, pl.ds(z * s.zp, s.zp)]
        mine[...] = reduced.astype(BF16)
        for d in far_first(s.nz):
            send(mine, mine, m["zg_ss"].at[it], m["zg_rs"].at[it], along_z(d))
        await_bytes(m["sz_recv"].at[it], m["sz_rs"].at[it])
        norm2 = from_row(m["sz_send"][it] + jnp.sum(m["sz_recv"][it], axis=0), n)
        return norm2

    def predicted(it):
        return [
            m["f_all"][it, j * s.groups : (j + 1) * s.groups].astype(F32).reshape(n, LANE) for j in range(s.fb)
        ]

    def gathered(it):
        await_bytes(m["f_recv"].at[it], m["zg_rs"].at[it])
        return predicted(it)

    sum_start(0, row_sums(lane_blocks(observed)))
    w1 = adjoint(0, observed.astype(BF16))
    m["w1"][...] = w1
    norm2 = forward(0, w1)
    beta1 = jnp.sqrt(sum_end(0) + EPSILON)
    alpha1 = jnp.sqrt(norm2 / (beta1 * beta1) + EPSILON)
    scale1 = 1.0 / (beta1 * alpha1)
    ratio = alpha1 / beta1
    seen = lane_blocks(misfit[...])
    left = [f * scale1 - ratio * o for f, o in zip(gathered(0), seen, strict=True)]

    sum_start(1, row_sums(left))
    w2 = adjoint(1, jnp.concatenate(left, axis=1).astype(BF16))
    beta2 = jnp.sqrt(sum_end(1) + EPSILON)
    m["coef"][0] = (1.0 / beta2).reshape(s.groups, TILE, LANE)
    m["coef"][1] = (beta2 * scale1).reshape(s.groups, TILE, LANE)
    share = []
    for i in range(s.tp):
        group = lax.rem(y * s.tp + i, s.groups)
        share.append(w2[i] * m["coef"][0, group] - m["w1"][i] * m["coef"][1, group])
    norm2 = forward(1, jnp.stack(share, axis=0))
    alpha2 = jnp.sqrt(norm2 + EPSILON)
    inverse2 = 1.0 / alpha2
    ratio = alpha2 / beta2
    left = [f * inverse2 - ratio * o for f, o in zip(gathered(1), left, strict=True)]

    sum_start(2, row_sums(left))
    rho1 = jnp.sqrt(alpha1 * alpha1 + beta2 * beta2)
    cosine, sine = alpha1 / rho1, beta2 / rho1
    phi1 = cosine * beta1
    phibar = sine * beta1
    theta = sine * alpha2
    rhobar = -cosine * alpha2

    first = place * (s.width // s.rows)
    block = first // LANE
    lane = lax.rem(first, LANE)
    share_width = s.width // s.rows
    cover = -(-share_width // LANE)
    shape = ((cover + 1) * LANE, cover * LANE)
    pick = lax.broadcasted_iota(jnp.int32, shape, 0) == lax.broadcasted_iota(jnp.int32, shape, 1) + lane
    pick = jnp.where(pick, 1.0, 0.0).astype(BF16)
    window = []
    for it in range(2):
        sides = []
        for k in range(cover + 1):
            b = jnp.minimum(block + k, s.width // LANE - 1)
            sides.append(m["v"][it, b // s.nb, pl.ds(lax.rem(b, s.nb) * s.groups, s.groups)].reshape(n, LANE))
        window.append(jnp.dot(jnp.concatenate(sides, axis=1), pick, preferred_element_type=F32))

    sum_middle(2)
    beta3 = jnp.sqrt(sum_end(2) + EPSILON)
    rho2 = jnp.sqrt(rhobar * rhobar + beta3 * beta3)
    phi2 = rhobar / rho2 * phibar
    on2 = phi2 / rho2
    weight1 = (phi1 / rho1 - on2 * (theta / rho1)) * scale1
    weight2 = on2 * inverse2
    result = [weight1 * a + weight2 * b for a, b in zip(lane_blocks(window[0]), lane_blocks(window[1]), strict=True)]
    slip[...] = jnp.concatenate(result, axis=1)[:, 0:share_width]
    for j, (f1, f2, o) in enumerate(zip(predicted(0), predicted(1), seen, strict=True)):
        misfit[:, j * LANE : (j + 1) * LANE] = o - weight1 * f1 - weight2 * f2

    await_bytes(m["halo"], m["halo_ss"].at[0])
    for it in range(2):
        await_bytes(m["pc_send"].at[it], m["c_ss"].at[it])
        await_bytes(m["px_send"].at[it], m["x_ss"].at[it])
        await_bytes(m["q_recv"].at[it], m["y_ss"].at[it])
        await_bytes(m["q_recv"].at[it], m["yg_ss"].at[it])
        await_bytes(m["px_send"].at[it], m["xg_ss"].at[it])
        await_bytes(m["pc_send"].at[it], m["cg_ss"].at[it])
        await_bytes(m["f_recv"].at[it], m["z_ss"].at[it])
        await_bytes(m["f_recv"].at[it], m["zg_ss"].at[it])
        await_bytes(m["sz_recv"].at[it], m["sz_ss"].at[it])
    for i in range(3):
        await_bytes(m["sa_recv"].at[i], m["sa_ss"].at[i])
        await_bytes(m["sb_recv"].at[i], m["sb_ss"].at[i])


def body(dims, nz, data, source, near_tiles, near_rows, near_cols, near_count, far_left, far_right):
    realiz, pixels = data.shape
    rank, width = far_right.shape
    slots, tile_rows, tile_cols = near_tiles.shape
    s = Sizes(dims, nz, realiz, pixels, width, slots, rank, tile_rows, tile_cols)
    per_row = width // tile_cols
    positions = pixels // tile_rows * per_row
    slot = jnp.arange(slots, dtype=jnp.int32)
    where = jnp.where(slot < near_count[0, 0], near_rows[:, 0] * per_row + near_cols[:, 0], -1)
    found = where[None, :] == jnp.arange(positions, dtype=jnp.int32)[:, None]
    slot_of = jnp.sum(jnp.where(found, slot[None, :], 0), axis=1)
    live = jnp.sum(jnp.where(found, 1.0, 0.0), axis=1)
    vmem = pl.BlockSpec(memory_space=pltpu.VMEM)
    smem = pl.BlockSpec(memory_space=pltpu.SMEM)
    return pl.pallas_call(
        functools.partial(kernel, s),
        out_shape=(
            jax.ShapeDtypeStruct((realiz, width // s.rows), F32),
            jax.ShapeDtypeStruct((realiz, pixels), F32),
        ),
        in_specs=[vmem, vmem, smem, smem, pl.BlockSpec(memory_space=pl.ANY), vmem, vmem],
        out_specs=(vmem, vmem),
        scratch_shapes=scratch_shapes(s),
        compiler_params=pltpu.CompilerParams(
            collective_id=0, has_side_effects=True, vmem_limit_bytes=48 * 1024 * 1024
        ),
    )(data, source.reshape(1, pixels), slot_of, live, near_tiles, far_left, far_right)


def solution(mesh, dims=(4, 8, 2)):
    return jax.shard_map(
        functools.partial(body, dims, mesh.shape["cols"]),
        mesh=mesh,
        in_specs=(
            P(None, "rows"),
            P("rows"),
            P("rows", "cols", None),
            P("rows", "cols"),
            P("rows", "cols"),
            P("rows", "cols"),
            P("cols", "rows"),
            P("rows", "cols"),
        ),
        out_specs=(P(None, ("cols", "rows")), P(None, "rows")),
        check_vma=False,
    )
```

```python
import functools

import jax
import jax.numpy as jnp
from jax import lax
from jax.experimental import pallas as pl
from jax.experimental.pallas import tpu as pltpu
from jax.sharding import PartitionSpec as P

EPSILON = 1e-06
LANE = 128
TILE = 16
MESH = pl.DeviceIdType.MESH
F32 = jnp.float32
BF16 = jnp.bfloat16


class Part:
    def __init__(self, first, blocks, groups, ny):
        self.lanes = slice(first * LANE, (first + blocks) * LANE)
        self.blocks = blocks
        self.tb = blocks * groups
        self.tp = -(-self.tb // ny)
        self.tq = self.tp * ny
        self.half = (self.tb + 1) // 2


class Sizes:
    def __init__(self, dims, nz, realiz, pixels, width, slots, rank, tile_rows, tile_cols):
        self.nx, self.ny, self.cores = dims
        self.nz = nz
        self.rows = self.nx * self.ny * self.cores
        self.nq = self.nx * self.cores
        self.realiz, self.pixels, self.width = realiz, pixels, width
        self.slots, self.rank, self.tile_rows, self.tile_cols = slots, rank, tile_rows, tile_cols
        self.groups = realiz // TILE
        self.chunk = width // self.nq
        self.nb = self.chunk // LANE
        self.cut = (self.nb + 1) // 2
        self.parts = [
            Part(0, self.cut, self.groups, self.ny),
            Part(self.cut, self.nb - self.cut, self.groups, self.ny),
        ]
        self.tb = max(p.tb for p in self.parts)
        self.tp = max(p.tp for p in self.parts)
        self.tq = max(p.tq for p in self.parts)
        self.fb = pixels // LANE
        self.ft = self.fb * self.groups
        self.zp = -(-self.ft // nz)
        self.fz = self.zp * nz


def scratch_shapes(s):
    dma = pltpu.SemaphoreType.DMA
    tile = (TILE, LANE)
    return [
        pltpu.VMEM((s.realiz, s.pixels), F32),
        pltpu.VMEM((1, s.pixels), jnp.int32),
        pltpu.VMEM((s.slots, s.tile_rows, s.tile_cols), BF16),
        pltpu.VMEM((s.rank, s.pixels), BF16),
        pltpu.VMEM((s.rank, s.width), BF16),
        pltpu.SMEM((s.slots,), jnp.int32),
        pltpu.SMEM((s.slots,), jnp.int32),
        pltpu.SMEM((1, 1), jnp.int32),
        pltpu.VMEM((8, LANE), jnp.int32),
        pltpu.SMEM((8, LANE), jnp.int32),
        pltpu.VMEM((2, s.realiz, s.pixels), F32),
        pltpu.VMEM((3, s.pixels, s.pixels), BF16),
        pltpu.VMEM((s.nq, s.pixels, s.chunk), BF16),
        pltpu.VMEM((2, 2, s.nx, s.tb, *tile), BF16),
        pltpu.VMEM((2, 2, s.nx, s.tb, *tile), BF16),
        pltpu.VMEM((2, 2, 3, s.tb, *tile), BF16),
        pltpu.VMEM((2, 2, 3, s.tb, *tile), BF16),
        pltpu.VMEM((2, 2, s.tq, *tile), BF16),
        pltpu.VMEM((2, 2, s.ny - 1, s.tp, *tile), BF16),
        pltpu.VMEM((2, s.nq, 2, s.tq, *tile), BF16),
        pltpu.VMEM((2, s.fz, *tile), BF16),
        pltpu.VMEM((2, s.nz - 1, s.zp, *tile), BF16),
        pltpu.VMEM((2, s.fz, *tile), BF16),
        pltpu.VMEM((2, s.tp, *tile), F32),
        pltpu.VMEM((2, s.groups, *tile), F32),
        pltpu.VMEM((3, 8, LANE), F32),
        pltpu.VMEM((3, s.nq - 1, 8, LANE), F32),
        pltpu.VMEM((3, 8, LANE), F32),
        pltpu.VMEM((3, s.ny - 1, 8, LANE), F32),
        pltpu.VMEM((2, 8, LANE), F32),
        pltpu.VMEM((2, s.nz - 1, 8, LANE), F32),
        dma((9,)),
        dma((1,)),
        dma((2,)),
        dma((2, 2)),
        dma((2, 2, s.nx)),
        dma((2, 2)),
        dma((2, 2, 4)),
        dma((2, 2)),
        dma((2, 2)),
        dma((2, 2)),
        dma((2, 2)),
        dma((2, 2)),
        dma((2, 2, 4)),
        dma((2, 2)),
        dma((2, 2, 5)),
        dma((2,)),
        dma((2,)),
        dma((2,)),
        dma((2,)),
        dma((3,)),
        dma((3,)),
        dma((3,)),
        dma((3,)),
        dma((2,)),
        dma((2,)),
    ]


def far_first(count):
    return sorted(range(1, count), key=lambda d: (-min(d, count - d), d))


def near_first(count):
    return sorted(range(1, count), key=lambda d: (min(d, count - d), d))


def await_bytes(ref, sem):
    pltpu.make_async_copy(ref, ref, sem).wait()


def to_row(column):
    rows = column.shape[0]
    wide = jnp.broadcast_to(column, (rows, LANE))
    wide = jnp.concatenate([wide, jnp.zeros((LANE - rows, LANE), F32)], axis=0)
    return wide.T[0:8]


def from_row(row, rows):
    return jnp.broadcast_to(row[0:1], (LANE, LANE)).T[0:rows]


def row_sums(blocks):
    total = blocks[0] * blocks[0]
    for block in blocks[1:]:
        total = total + block * block
    return jnp.sum(total, axis=1, keepdims=True)


def lane_blocks(value):
    return [value[:, j * LANE : (j + 1) * LANE] for j in range(value.shape[1] // LANE)]


def as_tiles(value):
    groups = value.shape[0] // TILE
    return jnp.concatenate([b.reshape(groups, TILE, LANE) for b in lane_blocks(value)], axis=0)


def from_tiles(tiles, groups):
    count = tiles.shape[0] // groups
    return jnp.concatenate(
        [tiles[j * groups : (j + 1) * groups].reshape(groups * TILE, LANE) for j in range(count)], axis=1
    )


def three_parts(value):
    high = value.astype(BF16)
    rest = value - high.astype(F32)
    middle = rest.astype(BF16)
    low = (rest - middle.astype(F32)).astype(BF16)
    return jnp.concatenate([high, middle, low], axis=0)


def kernel(
    s, data_hbm, source_hbm, rows_hbm, cols_hbm, count_hbm, tiles_hbm, left_hbm, right_hbm, slip, misfit,
    data, source, tiles, far_left, far_right, near_rows, near_cols, near_count, table, table_s, halo, onehot, g,
    pc_send, pc_recv, px_send, px_recv, q_send, q_recv, v, f_send, f_recv, f_all, w1, coef, sa_send, sa_recv,
    sb_send, sb_recv, sz_send, sz_recv, in_sem, halo_ss, halo_rs, c_ss, c_rs, x_ss, x_rs, y_ss, y_rs, yg_ss,
    yg_rs, xg_ss, xg_rs, cg_ss, cg_rs, z_ss, z_rs, zg_ss, zg_rs, sa_ss, sa_rs, sb_ss, sb_rs, sz_ss, sz_rs,
):
    place = lax.axis_index("rows")
    z = lax.axis_index("cols")
    core = lax.rem(place, 2)
    chip = place // 2
    y = lax.rem(chip, s.ny)
    x = chip // s.ny
    other = 1 - core
    own_q = core * s.nx + x
    n = s.realiz

    def at(xx, yy, cc):
        return ((xx * s.ny + yy) * 2 + cc, z)

    def cross(d):
        q = lax.rem(own_q + d, s.nq)
        return at(lax.rem(q, s.nx), y, q // s.nx)

    def along_y(d):
        return at(x, lax.rem(y + d, s.ny), core)

    def along_z(d):
        return (place, lax.rem(z + d, s.nz))

    def beside(d):
        return lax.rem(x + d + s.nx, s.nx)

    mate = at(x, y, other)
    up = at(beside(1), y, core)
    down = at(beside(-1), y, core)

    def send(src, dst, send_sem, recv_sem, device):
        pltpu.make_async_remote_copy(
            src_ref=src, dst_ref=dst, send_sem=send_sem, recv_sem=recv_sem, device_id=device, device_id_type=MESH
        ).start()

    pairs = [
        (rows_hbm, near_rows),
        (cols_hbm, near_cols),
        (count_hbm, near_count),
        (source_hbm, source),
        (data_hbm, data),
        (left_hbm, far_left),
        (right_hbm, far_right),
        (tiles_hbm, tiles),
    ]
    loads = [pltpu.make_async_copy(src, dst, in_sem.at[k]) for k, (src, dst) in enumerate(pairs)]
    for load in loads:
        load.start()

    step_out = lax.rem(place + s.rows + 2 * core - 1, s.rows)
    partners = [cross(d) for d in range(1, s.nq)]
    partners += [along_y(d) for d in range(1, s.ny)]
    partners += [along_z(d) for d in range(1, s.nz)]
    partners += [(step_out, z)]
    barrier = pltpu.get_barrier_semaphore()
    for device in partners:
        pl.semaphore_signal(barrier, inc=1, device_id=device, device_id_type=MESH)

    for load in loads[:3]:
        load.wait()
    per_row = s.width // s.tile_cols
    spot = lax.broadcasted_iota(jnp.int32, (8, LANE), 1)
    slot_of = jnp.full((8, LANE), -1, jnp.int32)
    for k in range(s.slots):
        where = jnp.where(k < near_count[0, 0], near_rows[k] * per_row + near_cols[k], -1)
        slot_of = jnp.where(spot == where, k, slot_of)
    table[...] = slot_of
    to_scalars = pltpu.make_async_copy(table, table_s, in_sem.at[8])
    to_scalars.start()

    pl.semaphore_wait(barrier, len(partners))

    after = lax.rem(place + 1, s.rows)
    before = lax.rem(place + s.rows - 1, s.rows)
    loads[4].wait()
    send(data, halo.at[0], halo_ss.at[0], halo_rs.at[0], (after, z))
    send(data, halo.at[1], halo_ss.at[0], halo_rs.at[1], (before, z))

    loads[3].wait()
    total = s.rows * s.pixels
    offset = source[...] + s.pixels - place * s.pixels
    offset = jnp.where(offset < 0, offset + total, offset)
    offset = jnp.where(offset >= total, offset - total, offset)
    index = lax.broadcasted_iota(jnp.int32, (s.pixels, s.pixels), 0)
    for k in range(3):
        onehot[k] = jnp.where(index == offset - k * s.pixels, 1.0, 0.0).astype(BF16)

    for load in loads[5:]:
        load.wait()
    to_scalars.wait()
    half = per_row // 2
    half_blocks = half * s.tile_cols // LANE
    bands = s.pixels // s.tile_rows

    def build(i, carry):
        side, a = i // bands, lax.rem(i, bands)
        pixel = pl.ds(pl.multiple_of(a * s.tile_rows, s.tile_rows), s.tile_rows)
        lefts = far_left[:, pixel]
        for b in range(half):
            column = pl.ds(pl.multiple_of((side * half + b) * s.tile_cols, s.tile_cols), s.tile_cols)
            block = lax.dot_general(lefts, far_right[:, column], (((0,), (0,)), ((), ())), preferred_element_type=F32)
            slot = table_s[0, a * per_row + side * half + b]
            near = tiles[jnp.maximum(slot, 0)].astype(F32)
            block = (block + near * jnp.where(slot >= 0, 1.0, 0.0)).astype(BF16)
            for k in range(s.tile_cols // LANE):
                j = b * (s.tile_cols // LANE) + k
                q = side * (half_blocks // s.nb) + j // s.nb
                lane = (j % s.nb) * LANE
                g[q, pixel, lane : lane + LANE] = block[:, k * LANE : (k + 1) * LANE]
        return carry

    lax.fori_loop(0, 2 * bands, build, 0)

    seen = jnp.dot(three_parts(data[...]), onehot[1], preferred_element_type=F32)
    for k in range(2):
        await_bytes(halo.at[k], halo_rs.at[k])
        seen = seen + jnp.dot(three_parts(halo[k]), onehot[2 * k], preferred_element_type=F32)
    observed = (seen[0:n] + seen[n : 2 * n]) + seen[2 * n : 3 * n]
    misfit[...] = observed

    def sum_start(i, column):
        sa_send[i] = to_row(column)
        for d in range(1, s.nq):
            send(sa_send.at[i], sa_recv.at[i, d - 1], sa_ss.at[i], sa_rs.at[i], cross(d))

    def sum_middle(i):
        await_bytes(sa_recv.at[i], sa_rs.at[i])
        sb_send[i] = sa_send[i] + jnp.sum(sa_recv[i], axis=0)
        for d in range(1, s.ny):
            send(sb_send.at[i], sb_recv.at[i, d - 1], sb_ss.at[i], sb_rs.at[i], along_y(d))

    def sum_end(i):
        await_bytes(sb_recv.at[i], sb_rs.at[i])
        return from_row(sb_send[i] + jnp.sum(sb_recv[i], axis=0), n)

    def adjoint(it, pixel_b, column):
        def product(q, p):
            return as_tiles(jnp.dot(pixel_b, g[q, :, s.parts[p].lanes], preferred_element_type=F32))

        def to_mate(d, p):
            tb = s.parts[p].tb
            mine = pc_send.at[it, p, d, 0:tb]
            mine[...] = product(other * s.nx + beside(d), p).astype(BF16)
            send(mine, pc_recv.at[it, p, d, 0:tb], c_ss.at[it, p], c_rs.at[it, p, d], mate)

        def pair_sum(d, p):
            own = product(core * s.nx + beside(d), p)
            came = pc_recv.at[it, p, d, 0 : s.parts[p].tb]
            await_bytes(came, c_rs.at[it, p, d])
            return own + came[...].astype(F32)

        def relay_out(p):
            tb, cut = s.parts[p].tb, s.parts[p].half
            px_send[it, p, 0, 0:tb] = pair_sum(2, p).astype(BF16)
            for k, (lo, hi, device) in enumerate(((0, cut, up), (cut, tb, down))):
                send(
                    px_send.at[it, p, 0, lo:hi],
                    px_recv.at[it, p, 2, lo:hi],
                    x_ss.at[it, p],
                    x_rs.at[it, p, 2 + k],
                    device,
                )

        def relay_on(k, p):
            tb, cut = s.parts[p].tb, s.parts[p].half
            lo, hi = ((0, cut), (cut, tb))[k]
            own = pair_sum((1, 3)[k], p)
            came = px_recv.at[it, p, 2, lo:hi]
            await_bytes(came, x_rs.at[it, p, 2 + k])
            passed = own[lo:hi] + came[...].astype(F32)
            own = jnp.concatenate([passed, own[hi:]] if k == 0 else [own[:lo], passed], axis=0)
            px_send[it, p, 1 + k, 0:tb] = own.astype(BF16)
            send(
                px_send.at[it, p, 1 + k, 0:tb],
                px_recv.at[it, p, k, 0:tb],
                x_ss.at[it, p],
                x_rs.at[it, p, k],
                (up, down)[k],
            )

        def scatter_y(p):
            tb, tp, tq = s.parts[p].tb, s.parts[p].tp, s.parts[p].tq
            own = pair_sum(0, p)
            for k in range(2):
                came = px_recv.at[it, p, k, 0:tb]
                await_bytes(came, x_rs.at[it, p, k])
                own = own + came[...].astype(F32)
            q_send[it, p, 0:tb] = own.astype(BF16)
            if tq > tb:
                q_send[it, p, tb:tq] = jnp.zeros((tq - tb, TILE, LANE), BF16)
            for d in far_first(s.ny):
                piece = pl.ds(lax.rem(y + d, s.ny) * tp, tp)
                send(
                    q_send.at[it, p, piece],
                    q_recv.at[it, p, d - 1, 0:tp],
                    y_ss.at[it, p],
                    y_rs.at[it, p],
                    along_y(d),
                )

        to_mate(2, 0)
        to_mate(2, 1)
        to_mate(1, 0)
        to_mate(3, 0)
        relay_out(0)
        relay_out(1)
        sum_start(it, column)
        to_mate(1, 1)
        to_mate(3, 1)
        relay_on(0, 0)
        relay_on(1, 0)
        to_mate(0, 0)
        to_mate(0, 1)
        relay_on(0, 1)
        relay_on(1, 1)
        sum_middle(it)
        scatter_y(0)
        scatter_y(1)

    def y_share(it, p):
        tp = s.parts[p].tp
        await_bytes(q_recv.at[it, p, :, 0:tp], y_rs.at[it, p])
        share = q_send[it, p, pl.ds(y * tp, tp)].astype(F32)
        for d in range(s.ny - 1):
            share = share + q_recv[it, p, d, 0:tp].astype(F32)
        return share

    def spread_y(it, p, share):
        tp = s.parts[p].tp
        mine = v.at[it, own_q, p, pl.ds(y * tp, tp)]
        mine[...] = share.astype(BF16)
        for d in far_first(s.ny):
            send(mine, mine, yg_ss.at[it, p], yg_rs.at[it, p], along_y(d))

    def forward(it):
        def product(q, p):
            return lax.dot_general(
                from_tiles(v[it, q, p, 0 : s.parts[p].tb], s.groups),
                g[q, :, s.parts[p].lanes],
                (((1,), (1,)), ((), ())),
                preferred_element_type=F32,
            )

        def pass_x(q, p, lo, hi, k, device):
            piece = v.at[it, q, p, lo:hi]
            send(piece, piece, xg_ss.at[it, p], xg_rs.at[it, p, k], device)

        def pass_mate(q, p, lo, hi, k):
            piece = v.at[it, q, p, lo:hi]
            send(piece, piece, cg_ss.at[it, p], cg_rs.at[it, p, k], mate)

        total = jnp.zeros((n, s.pixels), F32)
        for p, part in enumerate(s.parts):
            await_bytes(q_recv.at[it, p, :, 0 : part.tp], yg_rs.at[it, p])
            pass_x(own_q, p, 0, part.tb, 0, up)
            pass_x(own_q, p, 0, part.tb, 1, down)
            pass_mate(own_q, p, 0, part.tb, 0)
            total = total + product(own_q, p)
        for p, part in enumerate(s.parts):
            for k in range(2):
                q = core * s.nx + beside((-1, 1)[k])
                lo, hi = ((0, part.half), (part.half, part.tb))[k]
                await_bytes(v.at[it, q, p, 0 : part.tb], xg_rs.at[it, p, k])
                pass_x(q, p, lo, hi, 2 + k, (up, down)[k])
                pass_mate(q, p, 0, part.tb, 1 + k)
                total = total + product(q, p)
        q = core * s.nx + beside(2)
        for p, part in enumerate(s.parts):
            for k in range(2):
                lo, hi = ((0, part.half), (part.half, part.tb))[k]
                await_bytes(v.at[it, q, p, lo:hi], xg_rs.at[it, p, 2 + k])
                pass_mate(q, p, lo, hi, 3 + k)
            total = total + product(q, p)
        for d in (0, -1, 1, 2):
            q = other * s.nx + beside(d)
            for p, part in enumerate(s.parts):
                if d == 2:
                    await_bytes(v.at[it, q, p, 0 : part.half], cg_rs.at[it, p, 3])
                    await_bytes(v.at[it, q, p, part.half : part.tb], cg_rs.at[it, p, 4])
                else:
                    await_bytes(v.at[it, q, p, 0 : part.tb], cg_rs.at[it, p, (0, 2, 1)[d]])
                total = total + product(q, p)

        f_send[it, 0 : s.ft] = as_tiles(total).astype(BF16)
        if s.fz > s.ft:
            f_send[it, s.ft : s.fz] = jnp.zeros((s.fz - s.ft, TILE, LANE), BF16)
        for d in far_first(s.nz):
            piece = pl.ds(lax.rem(z + d, s.nz) * s.zp, s.zp)
            send(f_send.at[it, piece], f_recv.at[it, d - 1], z_ss.at[it], z_rs.at[it], along_z(d))

        def squares(q, running):
            for p, part in enumerate(s.parts):
                for j in range(part.blocks):
                    block = v[it, q, p, j * s.groups : (j + 1) * s.groups].astype(F32).reshape(n, LANE)
                    running = running + block * block
            return running

        running = lax.fori_loop(0, s.nq, squares, jnp.zeros((n, LANE), F32))
        sz_send[it] = to_row(jnp.sum(running, axis=1, keepdims=True))
        for d in far_first(s.nz):
            send(sz_send.at[it], sz_recv.at[it, d - 1], sz_ss.at[it], sz_rs.at[it], along_z(d))

        await_bytes(f_recv.at[it], z_rs.at[it])
        reduced = f_send[it, pl.ds(z * s.zp, s.zp)].astype(F32)
        for d in range(s.nz - 1):
            reduced = reduced + f_recv[it, d].astype(F32)
        mine = f_all.at[it, pl.ds(z * s.zp, s.zp)]
        mine[...] = reduced.astype(BF16)
        for d in far_first(s.nz):
            send(mine, mine, zg_ss.at[it], zg_rs.at[it], along_z(d))
        await_bytes(sz_recv.at[it], sz_rs.at[it])
        return from_row(sz_send[it] + jnp.sum(sz_recv[it], axis=0), n)

    def predicted(it):
        return [f_all[it, j * s.groups : (j + 1) * s.groups].astype(F32).reshape(n, LANE) for j in range(s.fb)]

    def gathered(it):
        await_bytes(f_recv.at[it], zg_rs.at[it])
        return predicted(it)

    adjoint(0, observed.astype(BF16), row_sums(lane_blocks(observed)))
    for p, part in enumerate(s.parts):
        share = y_share(0, p)
        spread_y(0, p, share)
        w1[p, 0 : part.tp] = share
    norm2 = forward(0)
    beta1 = jnp.sqrt(sum_end(0) + EPSILON)
    alpha1 = jnp.sqrt(norm2 / (beta1 * beta1) + EPSILON)
    scale1 = 1.0 / (beta1 * alpha1)
    ratio = alpha1 / beta1
    seen = lane_blocks(misfit[...])
    left = [f * scale1 - ratio * o for f, o in zip(gathered(0), seen, strict=True)]

    adjoint(1, jnp.concatenate(left, axis=1).astype(BF16), row_sums(left))
    beta2 = jnp.sqrt(sum_end(1) + EPSILON)
    coef[0] = (1.0 / beta2).reshape(s.groups, TILE, LANE)
    coef[1] = (beta2 * scale1).reshape(s.groups, TILE, LANE)
    for p, part in enumerate(s.parts):
        w2 = y_share(1, p)
        share = []
        for i in range(part.tp):
            group = lax.rem(y * part.tp + i, s.groups)
            share.append(w2[i] * coef[0, group] - w1[p, i] * coef[1, group])
        spread_y(1, p, jnp.stack(share, axis=0))
    norm2 = forward(1)
    alpha2 = jnp.sqrt(norm2 + EPSILON)
    inverse2 = 1.0 / alpha2
    ratio = alpha2 / beta2
    left = [f * inverse2 - ratio * o for f, o in zip(gathered(1), left, strict=True)]

    sum_start(2, row_sums(left))
    rho1 = jnp.sqrt(alpha1 * alpha1 + beta2 * beta2)
    cosine, sine = alpha1 / rho1, beta2 / rho1
    phi1 = cosine * beta1
    phibar = sine * beta1
    theta = sine * alpha2
    rhobar = -cosine * alpha2

    first = place * (s.width // s.rows)
    block = first // LANE
    lane = lax.rem(first, LANE)
    share_width = s.width // s.rows
    cover = -(-share_width // LANE)
    shape = ((cover + 1) * LANE, cover * LANE)
    pick = lax.broadcasted_iota(jnp.int32, shape, 0) == lax.broadcasted_iota(jnp.int32, shape, 1) + lane
    pick = jnp.where(pick, 1.0, 0.0).astype(BF16)
    window = []
    for it in range(2):
        sides = []
        for k in range(cover + 1):
            b = jnp.minimum(block + k, s.width // LANE - 1)
            j = lax.rem(b, s.nb)
            p = j // s.cut
            inside = (j - p * s.cut) * s.groups
            sides.append(v[it, b // s.nb, p, pl.ds(inside, s.groups)].reshape(n, LANE))
        window.append(jnp.dot(jnp.concatenate(sides, axis=1), pick, preferred_element_type=F32))

    sum_middle(2)
    beta3 = jnp.sqrt(sum_end(2) + EPSILON)
    rho2 = jnp.sqrt(rhobar * rhobar + beta3 * beta3)
    phi2 = rhobar / rho2 * phibar
    on2 = phi2 / rho2
    weight1 = (phi1 / rho1 - on2 * (theta / rho1)) * scale1
    weight2 = on2 * inverse2
    result = [weight1 * a + weight2 * b for a, b in zip(lane_blocks(window[0]), lane_blocks(window[1]), strict=True)]
    slip[...] = jnp.concatenate(result, axis=1)[:, 0:share_width]
    for j, (f1, f2, o) in enumerate(zip(predicted(0), predicted(1), seen, strict=True)):
        misfit[:, j * LANE : (j + 1) * LANE] = o - weight1 * f1 - weight2 * f2

    await_bytes(halo, halo_ss.at[0])
    for it in range(2):
        for p, part in enumerate(s.parts):
            four = pc_send.at[it, p, :, 0 : part.tb]
            three = px_send.at[it, p, :, 0 : part.tb]
            pieces = q_recv.at[it, p, :, 0 : part.tp]
            await_bytes(four, c_ss.at[it, p])
            await_bytes(three, x_ss.at[it, p])
            await_bytes(pieces, y_ss.at[it, p])
            await_bytes(pieces, yg_ss.at[it, p])
            await_bytes(three, xg_ss.at[it, p])
            await_bytes(four, cg_ss.at[it, p])
        await_bytes(f_recv.at[it], z_ss.at[it])
        await_bytes(f_recv.at[it], zg_ss.at[it])
        await_bytes(sz_recv.at[it], sz_ss.at[it])
    for i in range(3):
        await_bytes(sa_recv.at[i], sa_ss.at[i])
        await_bytes(sb_recv.at[i], sb_ss.at[i])


def body(dims, nz, data, source, near_tiles, near_rows, near_cols, near_count, far_left, far_right):
    realiz, pixels = data.shape
    rank, width = far_right.shape
    slots, tile_rows, tile_cols = near_tiles.shape
    s = Sizes(dims, nz, realiz, pixels, width, slots, rank, tile_rows, tile_cols)
    vmem = pl.BlockSpec(memory_space=pltpu.VMEM)
    return pl.pallas_call(
        functools.partial(kernel, s),
        out_shape=(
            jax.ShapeDtypeStruct((realiz, width // s.rows), F32),
            jax.ShapeDtypeStruct((realiz, pixels), F32),
        ),
        in_specs=[pl.BlockSpec(memory_space=pl.ANY)] * 8,
        out_specs=(vmem, vmem),
        scratch_shapes=scratch_shapes(s),
        compiler_params=pltpu.CompilerParams(
            collective_id=0, has_side_effects=True, vmem_limit_bytes=58 * 1024 * 1024
        ),
    )(
        data,
        source.reshape(1, pixels),
        near_rows.reshape(slots),
        near_cols.reshape(slots),
        near_count,
        near_tiles,
        far_left,
        far_right,
    )


def solution(mesh, dims=(4, 8, 2)):
    return jax.shard_map(
        functools.partial(body, dims, mesh.shape["cols"]),
        mesh=mesh,
        in_specs=(
            P(None, "rows"),
            P("rows"),
            P("rows", "cols", None),
            P("rows", "cols"),
            P("rows", "cols"),
            P("rows", "cols"),
            P("cols", "rows"),
            P("rows", "cols"),
        ),
        out_specs=(P(None, ("cols", "rows")), P(None, "rows")),
        check_vma=False,
    )
```

```python
import functools

import jax
import jax.numpy as jnp
from jax import lax
from jax.experimental import pallas as pl
from jax.experimental.pallas import tpu as pltpu
from jax.sharding import PartitionSpec as P

EPSILON = 1e-06
LANE = 128
TILE = 16
MESH = pl.DeviceIdType.MESH
F32 = jnp.float32
BF16 = jnp.bfloat16


class Part:
    def __init__(self, first, groups, s):
        self.first, self.groups = first, groups
        self.rows = slice(first * TILE, (first + groups) * TILE)
        self.n = groups * TILE
        self.tb = s.nb * groups
        self.tp = -(-self.tb // s.ny)
        self.tq = self.tp * s.ny
        self.half = (self.tb + 1) // 2
        self.ft = s.fb * groups
        self.zp = -(-self.ft // s.nz)
        self.fz = self.zp * s.nz


class Sizes:
    def __init__(self, dims, nz, realiz, pixels, width, slots, rank, tile_rows, tile_cols):
        self.nx, self.ny, self.cores = dims
        self.nz = nz
        self.rows = self.nx * self.ny * self.cores
        self.nq = self.nx * self.cores
        self.realiz, self.pixels, self.width = realiz, pixels, width
        self.slots, self.rank, self.tile_rows, self.tile_cols = slots, rank, tile_rows, tile_cols
        self.groups = realiz // TILE
        self.chunk = width // self.nq
        self.nb = self.chunk // LANE
        self.fb = pixels // LANE
        cut = (self.groups + 1) // 2
        self.parts = [Part(0, cut, self), Part(cut, self.groups - cut, self)]
        for name in ("tb", "tp", "tq", "zp", "fz"):
            setattr(self, name, max(getattr(p, name) for p in self.parts))


def scratch_shapes(s):
    dma = pltpu.SemaphoreType.DMA
    tile = (TILE, LANE)
    return [
        pltpu.VMEM((s.realiz, s.pixels), F32),
        pltpu.VMEM((1, s.pixels), jnp.int32),
        pltpu.VMEM((s.slots, s.tile_rows, s.tile_cols), BF16),
        pltpu.VMEM((s.rank, s.pixels), BF16),
        pltpu.VMEM((s.rank, s.width), BF16),
        pltpu.SMEM((s.slots,), jnp.int32),
        pltpu.SMEM((s.slots,), jnp.int32),
        pltpu.SMEM((1, 1), jnp.int32),
        pltpu.VMEM((8, LANE), jnp.int32),
        pltpu.SMEM((8, LANE), jnp.int32),
        pltpu.VMEM((2, s.realiz, s.pixels), F32),
        pltpu.VMEM((3, s.pixels, s.pixels), BF16),
        pltpu.VMEM((s.nq, s.pixels, s.chunk), BF16),
        pltpu.VMEM((2, 2, s.nx, s.tb, *tile), BF16),
        pltpu.VMEM((2, 2, s.nx, s.tb, *tile), BF16),
        pltpu.VMEM((2, 2, 3, s.tb, *tile), BF16),
        pltpu.VMEM((2, 2, 3, s.tb, *tile), BF16),
        pltpu.VMEM((2, 2, s.tq, *tile), BF16),
        pltpu.VMEM((2, 2, s.ny - 1, s.tp, *tile), BF16),
        pltpu.VMEM((2, s.nq, 2, s.tq, *tile), BF16),
        pltpu.VMEM((2, 2, s.fz, *tile), BF16),
        pltpu.VMEM((2, 2, s.nz - 1, s.zp, *tile), BF16),
        pltpu.VMEM((2, 2, s.fz, *tile), BF16),
        pltpu.VMEM((s.realiz, s.pixels), F32),
        pltpu.VMEM((2, s.realiz, LANE), F32),
        pltpu.VMEM((2, s.realiz, LANE), F32),
        pltpu.VMEM((s.realiz, LANE), F32),
        pltpu.VMEM((2, s.tp, *tile), F32),
        pltpu.VMEM((2, s.groups, *tile), F32),
        pltpu.VMEM((3, 8, LANE), F32),
        pltpu.VMEM((3, s.nq - 1, 8, LANE), F32),
        pltpu.VMEM((3, 8, LANE), F32),
        pltpu.VMEM((3, s.ny - 1, 8, LANE), F32),
        pltpu.VMEM((2, 8, LANE), F32),
        pltpu.VMEM((2, s.nz - 1, 8, LANE), F32),
        dma((9,)),
        dma((1,)),
        dma((2,)),
        dma((2, 2)),
        dma((2, 2, s.nx)),
        dma((2, 2)),
        dma((2, 2, 4)),
        dma((2, 2)),
        dma((2, 2)),
        dma((2, 2)),
        dma((2, 2)),
        dma((2, 2)),
        dma((2, 2, 4)),
        dma((2, 2)),
        dma((2, 2, 5)),
        dma((2, 2)),
        dma((2, 2)),
        dma((2, 2)),
        dma((2, 2)),
        dma((3,)),
        dma((3,)),
        dma((3,)),
        dma((3,)),
        dma((2,)),
        dma((2,)),
    ]


def far_first(count):
    return sorted(range(1, count), key=lambda d: (-min(d, count - d), d))


def near_first(count):
    return sorted(range(1, count), key=lambda d: (min(d, count - d), d))


def await_bytes(ref, sem):
    pltpu.make_async_copy(ref, ref, sem).wait()


def to_row(column):
    rows = column.shape[0]
    wide = jnp.broadcast_to(column, (rows, LANE))
    wide = jnp.concatenate([wide, jnp.zeros((LANE - rows, LANE), F32)], axis=0)
    return wide.T[0:8]


def from_row(row, rows):
    return jnp.broadcast_to(row[0:1], (LANE, LANE)).T[0:rows]


def row_sums(blocks):
    total = blocks[0] * blocks[0]
    for block in blocks[1:]:
        total = total + block * block
    return jnp.sum(total, axis=1, keepdims=True)


def lane_blocks(value):
    return [value[:, j * LANE : (j + 1) * LANE] for j in range(value.shape[1] // LANE)]


def as_tiles(value):
    groups = value.shape[0] // TILE
    return jnp.concatenate([b.reshape(groups, TILE, LANE) for b in lane_blocks(value)], axis=0)


def from_tiles(tiles, groups):
    count = tiles.shape[0] // groups
    return jnp.concatenate(
        [tiles[j * groups : (j + 1) * groups].reshape(groups * TILE, LANE) for j in range(count)], axis=1
    )


def three_parts(value):
    high = value.astype(BF16)
    rest = value - high.astype(F32)
    middle = rest.astype(BF16)
    low = (rest - middle.astype(F32)).astype(BF16)
    return jnp.concatenate([high, middle, low], axis=0)


def kernel(
    s, data_hbm, source_hbm, rows_hbm, cols_hbm, count_hbm, tiles_hbm, left_hbm, right_hbm, slip, misfit,
    data, source, tiles, far_left, far_right, near_rows, near_cols, near_count, table, table_s, halo, onehot, g,
    pc_send, pc_recv, px_send, px_recv, q_send, q_recv, v, f_send, f_recv, f_all, left, alphas, betas, inverse,
    previous, coef, sa_send, sa_recv, sb_send, sb_recv, sz_send, sz_recv, in_sem, halo_ss, halo_rs, c_ss, c_rs,
    x_ss, x_rs, y_ss, y_rs, yg_ss, yg_rs, xg_ss, xg_rs, cg_ss, cg_rs, z_ss, z_rs, zg_ss, zg_rs, sa_ss, sa_rs,
    sb_ss, sb_rs, sz_ss, sz_rs,
):
    place = lax.axis_index("rows")
    z = lax.axis_index("cols")
    core = lax.rem(place, 2)
    chip = place // 2
    y = lax.rem(chip, s.ny)
    x = chip // s.ny
    other = 1 - core
    own_q = core * s.nx + x
    n = s.realiz

    def at(xx, yy, cc):
        return ((xx * s.ny + yy) * 2 + cc, z)

    def cross(d):
        q = lax.rem(own_q + d, s.nq)
        return at(lax.rem(q, s.nx), y, q // s.nx)

    def along_y(d):
        return at(x, lax.rem(y + d, s.ny), core)

    def along_z(d):
        return (place, lax.rem(z + d, s.nz))

    def beside(d):
        return lax.rem(x + d + s.nx, s.nx)

    mate = at(x, y, other)
    up = at(beside(1), y, core)
    down = at(beside(-1), y, core)

    def send(src, dst, send_sem, recv_sem, device):
        pltpu.make_async_remote_copy(
            src_ref=src, dst_ref=dst, send_sem=send_sem, recv_sem=recv_sem, device_id=device, device_id_type=MESH
        ).start()

    pairs = [
        (rows_hbm, near_rows),
        (cols_hbm, near_cols),
        (count_hbm, near_count),
        (source_hbm, source),
        (data_hbm, data),
        (left_hbm, far_left),
        (right_hbm, far_right),
        (tiles_hbm, tiles),
    ]
    loads = [pltpu.make_async_copy(src, dst, in_sem.at[k]) for k, (src, dst) in enumerate(pairs)]
    for load in loads:
        load.start()

    step_out = lax.rem(place + s.rows + 2 * core - 1, s.rows)
    partners = [cross(d) for d in range(1, s.nq)]
    partners += [along_y(d) for d in range(1, s.ny)]
    partners += [along_z(d) for d in range(1, s.nz)]
    partners += [(step_out, z)]
    barrier = pltpu.get_barrier_semaphore()
    for device in partners:
        pl.semaphore_signal(barrier, inc=1, device_id=device, device_id_type=MESH)

    for load in loads[:3]:
        load.wait()
    per_row = s.width // s.tile_cols
    spot = lax.broadcasted_iota(jnp.int32, (8, LANE), 1)
    slot_of = jnp.full((8, LANE), -1, jnp.int32)
    for k in range(s.slots):
        where = jnp.where(k < near_count[0, 0], near_rows[k] * per_row + near_cols[k], -1)
        slot_of = jnp.where(spot == where, k, slot_of)
    table[...] = slot_of
    to_scalars = pltpu.make_async_copy(table, table_s, in_sem.at[8])
    to_scalars.start()

    pl.semaphore_wait(barrier, len(partners))

    after = lax.rem(place + 1, s.rows)
    before = lax.rem(place + s.rows - 1, s.rows)
    loads[4].wait()
    send(data, halo.at[0], halo_ss.at[0], halo_rs.at[0], (after, z))
    send(data, halo.at[1], halo_ss.at[0], halo_rs.at[1], (before, z))

    loads[3].wait()
    total = s.rows * s.pixels
    offset = source[...] + s.pixels - place * s.pixels
    offset = jnp.where(offset < 0, offset + total, offset)
    offset = jnp.where(offset >= total, offset - total, offset)
    index = lax.broadcasted_iota(jnp.int32, (s.pixels, s.pixels), 0)
    for k in range(3):
        onehot[k] = jnp.where(index == offset - k * s.pixels, 1.0, 0.0).astype(BF16)

    for load in loads[5:]:
        load.wait()
    to_scalars.wait()
    half = per_row // 2
    half_blocks = half * s.tile_cols // LANE
    bands = s.pixels // s.tile_rows

    def build(i, carry):
        side, a = i // bands, lax.rem(i, bands)
        pixel = pl.ds(pl.multiple_of(a * s.tile_rows, s.tile_rows), s.tile_rows)
        lefts = far_left[:, pixel]
        for b in range(half):
            column = pl.ds(pl.multiple_of((side * half + b) * s.tile_cols, s.tile_cols), s.tile_cols)
            block = lax.dot_general(lefts, far_right[:, column], (((0,), (0,)), ((), ())), preferred_element_type=F32)
            slot = table_s[0, a * per_row + side * half + b]
            near = tiles[jnp.maximum(slot, 0)].astype(F32)
            block = (block + near * jnp.where(slot >= 0, 1.0, 0.0)).astype(BF16)
            for k in range(s.tile_cols // LANE):
                j = b * (s.tile_cols // LANE) + k
                q = side * (half_blocks // s.nb) + j // s.nb
                lane = (j % s.nb) * LANE
                g[q, pixel, lane : lane + LANE] = block[:, k * LANE : (k + 1) * LANE]
        return carry

    lax.fori_loop(0, 2 * bands, build, 0)

    seen = jnp.dot(three_parts(data[...]), onehot[1], preferred_element_type=F32)
    for k in range(2):
        await_bytes(halo.at[k], halo_rs.at[k])
        seen = seen + jnp.dot(three_parts(halo[k]), onehot[2 * k], preferred_element_type=F32)
    observed = (seen[0:n] + seen[n : 2 * n]) + seen[2 * n : 3 * n]
    misfit[...] = observed
    left[...] = observed
    previous[...] = jnp.zeros_like(previous)
    inverse[...] = jnp.zeros_like(inverse)

    def sum_start(i, column):
        sa_send[i] = to_row(column)
        for d in range(1, s.nq):
            send(sa_send.at[i], sa_recv.at[i, d - 1], sa_ss.at[i], sa_rs.at[i], cross(d))

    def sum_middle(i):
        await_bytes(sa_recv.at[i], sa_rs.at[i])
        sb_send[i] = sa_send[i] + jnp.sum(sa_recv[i], axis=0)
        for d in range(1, s.ny):
            send(sb_send.at[i], sb_recv.at[i, d - 1], sb_ss.at[i], sb_rs.at[i], along_y(d))

    def sum_end(i):
        await_bytes(sb_recv.at[i], sb_rs.at[i])
        return jnp.sqrt(from_row(sb_send[i] + jnp.sum(sb_recv[i], axis=0), n) + EPSILON)

    def pieces_of(p):
        return ((0, s.parts[p].half), (s.parts[p].half, s.parts[p].tb))

    def product(p, q):
        return as_tiles(jnp.dot(left[s.parts[p].rows, :].astype(BF16), g[q], preferred_element_type=F32))

    def to_mate(it, p):
        tb = s.parts[p].tb
        for d in (2, 1, 3, 0):
            mine = pc_send.at[it, p, d, 0:tb]
            mine[...] = product(p, other * s.nx + beside(d)).astype(BF16)
            send(mine, pc_recv.at[it, p, d, 0:tb], c_ss.at[it, p], c_rs.at[it, p, d], mate)

    def pair_sum(it, p, d):
        own = product(p, core * s.nx + beside(d))
        came = pc_recv.at[it, p, d, 0 : s.parts[p].tb]
        await_bytes(came, c_rs.at[it, p, d])
        return own + came[...].astype(F32)

    def relay_out(it, p):
        px_send[it, p, 0, 0 : s.parts[p].tb] = pair_sum(it, p, 2).astype(BF16)
        for k, (lo, hi) in enumerate(pieces_of(p)):
            send(
                px_send.at[it, p, 0, lo:hi],
                px_recv.at[it, p, 2, lo:hi],
                x_ss.at[it, p],
                x_rs.at[it, p, 2 + k],
                (up, down)[k],
            )

    def relay_on(it, p):
        tb = s.parts[p].tb
        for k, (lo, hi) in enumerate(pieces_of(p)):
            own = pair_sum(it, p, (1, 3)[k])
            came = px_recv.at[it, p, 2, lo:hi]
            await_bytes(came, x_rs.at[it, p, 2 + k])
            passed = own[lo:hi] + came[...].astype(F32)
            own = jnp.concatenate([passed, own[hi:]] if k == 0 else [own[:lo], passed], axis=0)
            px_send[it, p, 1 + k, 0:tb] = own.astype(BF16)
            send(
                px_send.at[it, p, 1 + k, 0:tb],
                px_recv.at[it, p, k, 0:tb],
                x_ss.at[it, p],
                x_rs.at[it, p, k],
                (up, down)[k],
            )

    def scatter_y(it, p):
        tb, tp, tq = s.parts[p].tb, s.parts[p].tp, s.parts[p].tq
        own = pair_sum(it, p, 0)
        for k in range(2):
            came = px_recv.at[it, p, k, 0:tb]
            await_bytes(came, x_rs.at[it, p, k])
            own = own + came[...].astype(F32)
        q_send[it, p, 0:tb] = own.astype(BF16)
        if tq > tb:
            q_send[it, p, tb:tq] = jnp.zeros((tq - tb, TILE, LANE), BF16)
        for d in far_first(s.ny):
            piece = pl.ds(lax.rem(y + d, s.ny) * tp, tp)
            send(q_send.at[it, p, piece], q_recv.at[it, p, d - 1, 0:tp], y_ss.at[it, p], y_rs.at[it, p], along_y(d))

    def spread_y(it, p):
        tp = s.parts[p].tp
        await_bytes(q_recv.at[it, p, :, 0:tp], y_rs.at[it, p])
        share = q_send[it, p, pl.ds(y * tp, tp)].astype(F32)
        for d in range(s.ny - 1):
            share = share + q_recv[it, p, d, 0:tp].astype(F32)
        mine = v.at[it, own_q, p, pl.ds(y * tp, tp)]
        for i in range(tp):
            group = s.parts[p].first + lax.rem(y * tp + i, s.parts[p].groups)
            raw = share[i] * coef[0, group] - previous[p, i] * coef[1, group]
            previous[p, i] = raw
            v[it, own_q, p, y * tp + i] = raw.astype(BF16)
        for d in far_first(s.ny):
            send(mine, mine, yg_ss.at[it, p], yg_rs.at[it, p], along_y(d))

    def applied(it, p, q):
        return lax.dot_general(
            from_tiles(v[it, q, p, 0 : s.parts[p].tb], s.parts[p].groups),
            g[q],
            (((1,), (1,)), ((), ())),
            preferred_element_type=F32,
        )

    def pass_x(it, p, q, lo, hi, k, device):
        piece = v.at[it, q, p, lo:hi]
        send(piece, piece, xg_ss.at[it, p], xg_rs.at[it, p, k], device)

    def pass_mate(it, p, q, lo, hi, k):
        piece = v.at[it, q, p, lo:hi]
        send(piece, piece, cg_ss.at[it, p], cg_rs.at[it, p, k], mate)

    def own_chunk(it, p):
        part = s.parts[p]
        await_bytes(q_recv.at[it, p, :, 0 : part.tp], yg_rs.at[it, p])
        pass_x(it, p, own_q, 0, part.tb, 0, up)
        pass_x(it, p, own_q, 0, part.tb, 1, down)
        pass_mate(it, p, own_q, 0, part.tb, 0)
        return applied(it, p, own_q)

    def next_chunks(it, p, total):
        part = s.parts[p]
        for k, (lo, hi) in enumerate(pieces_of(p)):
            q = core * s.nx + beside((-1, 1)[k])
            await_bytes(v.at[it, q, p, 0 : part.tb], xg_rs.at[it, p, k])
            pass_x(it, p, q, lo, hi, 2 + k, (up, down)[k])
            pass_mate(it, p, q, 0, part.tb, 1 + k)
        for d in (-1, 1):
            total = total + applied(it, p, core * s.nx + beside(d))
        q = other * s.nx + x
        await_bytes(v.at[it, q, p, 0 : part.tb], cg_rs.at[it, p, 0])
        return total + applied(it, p, q)

    def far_chunk(it, p, total):
        q = core * s.nx + beside(2)
        for k, (lo, hi) in enumerate(pieces_of(p)):
            await_bytes(v.at[it, q, p, lo:hi], xg_rs.at[it, p, 2 + k])
            pass_mate(it, p, q, lo, hi, 3 + k)
        total = total + applied(it, p, q)
        for d in (-1, 1):
            q = other * s.nx + beside(d)
            await_bytes(v.at[it, q, p, 0 : s.parts[p].tb], cg_rs.at[it, p, (0, 2, 1)[d]])
            total = total + applied(it, p, q)
        return total

    def scatter_z(it, p, total):
        part = s.parts[p]
        q = other * s.nx + beside(2)
        for k, (lo, hi) in enumerate(pieces_of(p)):
            await_bytes(v.at[it, q, p, lo:hi], cg_rs.at[it, p, 3 + k])
        total = total + applied(it, p, q)
        f_send[it, p, 0 : part.ft] = as_tiles(total).astype(BF16)
        if part.fz > part.ft:
            f_send[it, p, part.ft : part.fz] = jnp.zeros((part.fz - part.ft, TILE, LANE), BF16)
        for d in far_first(s.nz):
            piece = pl.ds(lax.rem(z + d, s.nz) * part.zp, part.zp)
            send(
                f_send.at[it, p, piece],
                f_recv.at[it, p, d - 1, 0 : part.zp],
                z_ss.at[it, p],
                z_rs.at[it, p],
                along_z(d),
            )

    def spread_z(it, p):
        zp = s.parts[p].zp
        await_bytes(f_recv.at[it, p, :, 0:zp], z_rs.at[it, p])
        reduced = f_send[it, p, pl.ds(z * zp, zp)].astype(F32)
        for d in range(s.nz - 1):
            reduced = reduced + f_recv[it, p, d, 0:zp].astype(F32)
        mine = f_all.at[it, p, pl.ds(z * zp, zp)]
        mine[...] = reduced.astype(BF16)
        for d in far_first(s.nz):
            send(mine, mine, zg_ss.at[it, p], zg_rs.at[it, p], along_z(d))

    def square_sums(it):
        sums = []
        for p, part in enumerate(s.parts):

            def squares(q, running, p=p, part=part):
                for j in range(s.nb):
                    block = v[it, q, p, j * part.groups : (j + 1) * part.groups].astype(F32).reshape(part.n, LANE)
                    running = running + block * block
                return running

            running = lax.fori_loop(0, s.nq, squares, jnp.zeros((part.n, LANE), F32))
            sums.append(jnp.sum(running, axis=1, keepdims=True))
        return jnp.concatenate(sums, axis=0)

    def predicted(it, p, j):
        part = s.parts[p]
        return f_all[it, p, j * part.groups : (j + 1) * part.groups].astype(F32).reshape(part.n, LANE)

    def left_sums():
        return row_sums(lane_blocks(left[...]))

    both = range(2)

    def iteration(it, carry):
        to_mate(it, 0)
        sum_start(it, left_sums())
        to_mate(it, 1)
        for p in both:
            relay_out(it, p)
        for p in both:
            relay_on(it, p)
        sum_middle(it)
        for p in both:
            scatter_y(it, p)
        beta = sum_end(it)
        betas[it] = beta
        coef[0] = (1.0 / beta).reshape(s.groups, TILE, LANE)
        coef[1] = (beta * inverse[...]).reshape(s.groups, TILE, LANE)
        for p in both:
            spread_y(it, p)
        total = [own_chunk(it, p) for p in both]
        total = [next_chunks(it, p, total[p]) for p in both]
        total = [far_chunk(it, p, total[p]) for p in both]
        for p in both:
            scatter_z(it, p, total[p])
        sz_send[it] = to_row(square_sums(it))
        for d in far_first(s.nz):
            send(sz_send.at[it], sz_recv.at[it, d - 1], sz_ss.at[it], sz_rs.at[it], along_z(d))
        for p in both:
            spread_z(it, p)
        await_bytes(sz_recv.at[it], sz_rs.at[it])
        alpha = jnp.sqrt(from_row(sz_send[it] + jnp.sum(sz_recv[it], axis=0), n) + EPSILON)
        alphas[it] = alpha
        inverse[...] = 1.0 / alpha
        ratio = alpha / beta
        for p, part in enumerate(s.parts):
            await_bytes(f_recv.at[it, p, :, 0 : part.zp], zg_rs.at[it, p])
            for j in range(s.fb):
                lanes = slice(j * LANE, (j + 1) * LANE)
                left[part.rows, lanes] = (
                    predicted(it, p, j) * inverse[part.rows] - left[part.rows, lanes] * ratio[part.rows]
                )
        return carry

    lax.fori_loop(0, 2, iteration, 0)

    sum_start(2, left_sums())
    alpha1, alpha2, beta1, beta2 = alphas[0], alphas[1], betas[0], betas[1]
    rho1 = jnp.sqrt(alpha1 * alpha1 + beta2 * beta2)
    cosine, sine = alpha1 / rho1, beta2 / rho1
    phi1 = cosine * beta1
    phibar = sine * beta1
    theta = sine * alpha2
    rhobar = -cosine * alpha2

    first = place * (s.width // s.rows)
    block = first // LANE
    lane = lax.rem(first, LANE)
    share_width = s.width // s.rows
    cover = -(-share_width // LANE)
    shape = ((cover + 1) * LANE, cover * LANE)
    pick = lax.broadcasted_iota(jnp.int32, shape, 0) == lax.broadcasted_iota(jnp.int32, shape, 1) + lane
    pick = jnp.where(pick, 1.0, 0.0).astype(BF16)
    window = []
    for it in range(2):
        sides = []
        for k in range(cover + 1):
            b = jnp.minimum(block + k, s.width // LANE - 1)
            j = lax.rem(b, s.nb)
            rows = [
                v[it, b // s.nb, p, pl.ds(j * part.groups, part.groups)].reshape(part.n, LANE)
                for p, part in enumerate(s.parts)
            ]
            sides.append(jnp.concatenate(rows, axis=0))
        window.append(jnp.dot(jnp.concatenate(sides, axis=1), pick, preferred_element_type=F32))

    sum_middle(2)
    beta3 = sum_end(2)
    rho2 = jnp.sqrt(rhobar * rhobar + beta3 * beta3)
    phi2 = rhobar / rho2 * phibar
    on2 = phi2 / rho2
    weight1 = (phi1 / rho1 - on2 * (theta / rho1)) / alpha1
    weight2 = on2 / alpha2
    result = [weight1 * a + weight2 * b for a, b in zip(lane_blocks(window[0]), lane_blocks(window[1]), strict=True)]
    slip[...] = jnp.concatenate(result, axis=1)[:, 0:share_width]
    for p, part in enumerate(s.parts):
        for j in range(s.fb):
            lanes = slice(j * LANE, (j + 1) * LANE)
            misfit[part.rows, lanes] = (
                misfit[part.rows, lanes]
                - weight1[part.rows] * predicted(0, p, j)
                - weight2[part.rows] * predicted(1, p, j)
            )

    await_bytes(halo, halo_ss.at[0])

    def settle(it, carry):
        for p, part in enumerate(s.parts):
            four = pc_send.at[it, p, :, 0 : part.tb]
            three = px_send.at[it, p, :, 0 : part.tb]
            pieces = q_recv.at[it, p, :, 0 : part.tp]
            fields = f_recv.at[it, p, :, 0 : part.zp]
            await_bytes(four, c_ss.at[it, p])
            await_bytes(three, x_ss.at[it, p])
            await_bytes(pieces, y_ss.at[it, p])
            await_bytes(pieces, yg_ss.at[it, p])
            await_bytes(three, xg_ss.at[it, p])
            await_bytes(four, cg_ss.at[it, p])
            await_bytes(fields, z_ss.at[it, p])
            await_bytes(fields, zg_ss.at[it, p])
        await_bytes(sz_recv.at[it], sz_ss.at[it])
        return carry

    lax.fori_loop(0, 2, settle, 0)
    for i in range(3):
        await_bytes(sa_recv.at[i], sa_ss.at[i])
        await_bytes(sb_recv.at[i], sb_ss.at[i])


def hand_over(slip_in, misfit_in, slip_out, misfit_out, sem):
    copies = [
        pltpu.make_async_copy(slip_in, slip_out, sem.at[0]),
        pltpu.make_async_copy(misfit_in, misfit_out, sem.at[1]),
    ]
    for copy in copies:
        copy.start()
    for copy in copies:
        copy.wait()


def body(dims, nz, data, source, near_tiles, near_rows, near_cols, near_count, far_left, far_right):
    realiz, pixels = data.shape
    rank, width = far_right.shape
    slots, tile_rows, tile_cols = near_tiles.shape
    s = Sizes(dims, nz, realiz, pixels, width, slots, rank, tile_rows, tile_cols)
    vmem = pl.BlockSpec(memory_space=pltpu.VMEM)
    out_shape = (
        jax.ShapeDtypeStruct((realiz, width // s.rows), F32),
        jax.ShapeDtypeStruct((realiz, pixels), F32),
    )
    results = pl.pallas_call(
        functools.partial(kernel, s),
        out_shape=out_shape,
        in_specs=[pl.BlockSpec(memory_space=pl.ANY)] * 8,
        out_specs=(vmem, vmem),
        scratch_shapes=scratch_shapes(s),
        compiler_params=pltpu.CompilerParams(
            collective_id=0, has_side_effects=True, vmem_limit_bytes=58 * 1024 * 1024
        ),
    )(
        data,
        source.reshape(1, pixels),
        near_rows.reshape(slots),
        near_cols.reshape(slots),
        near_count,
        near_tiles,
        far_left,
        far_right,
    )
    anywhere = pl.BlockSpec(memory_space=pl.ANY)
    return pl.pallas_call(
        hand_over,
        out_shape=out_shape,
        in_specs=[anywhere] * 2,
        out_specs=(anywhere, anywhere),
        scratch_shapes=[pltpu.SemaphoreType.DMA((2,))],
        compiler_params=pltpu.CompilerParams(vmem_limit_bytes=58 * 1024 * 1024),
    )(*results)


def solution(mesh, dims=(4, 8, 2)):
    return jax.shard_map(
        functools.partial(body, dims, mesh.shape["cols"]),
        mesh=mesh,
        in_specs=(
            P(None, "rows"),
            P("rows"),
            P("rows", "cols", None),
            P("rows", "cols"),
            P("rows", "cols"),
            P("rows", "cols"),
            P("cols", "rows"),
            P("rows", "cols"),
        ),
        out_specs=(P(None, ("cols", "rows")), P(None, "rows")),
        check_vma=False,
    )
```

```python
import functools

import jax
import jax.numpy as jnp
from jax import lax
from jax.experimental import pallas as pl
from jax.experimental.pallas import tpu as pltpu
from jax.sharding import PartitionSpec as P

EPSILON = 1e-06
LANE = 128
TILE = 16
MESH = pl.DeviceIdType.MESH
F32 = jnp.float32
BF16 = jnp.bfloat16


class Part:
    def __init__(self, first, blocks, s):
        self.lanes = slice(first * LANE, (first + blocks) * LANE)
        self.blocks = blocks
        self.tb = blocks * s.groups
        self.tp = -(-self.tb // s.ny)
        self.tq = self.tp * s.ny


class Sizes:
    def __init__(self, dims, nz, realiz, pixels, width, slots, rank, tile_rows, tile_cols):
        self.nx, self.ny, self.cores = dims
        self.nz = nz
        self.rows = self.nx * self.ny * self.cores
        self.nq = self.nx * self.cores
        self.realiz, self.pixels, self.width = realiz, pixels, width
        self.slots, self.rank, self.tile_rows, self.tile_cols = slots, rank, tile_rows, tile_cols
        self.groups = realiz // TILE
        self.chunk = width // self.nq
        self.nb = self.chunk // LANE
        self.fb = pixels // LANE
        self.ft = self.fb * self.groups
        self.zp = -(-self.ft // nz)
        self.fz = self.zp * nz
        self.cut = (self.nb + 1) // 2
        self.parts = [Part(0, self.cut, self), Part(self.cut, self.nb - self.cut, self)]
        self.tb = max(p.tb for p in self.parts)
        self.tp = max(p.tp for p in self.parts)
        self.tq = max(p.tq for p in self.parts)


def scratch_shapes(s):
    dma = pltpu.SemaphoreType.DMA
    tile = (TILE, LANE)
    return [
        pltpu.VMEM((s.realiz, s.pixels), F32),
        pltpu.VMEM((1, s.pixels), jnp.int32),
        pltpu.VMEM((s.slots, s.tile_rows, s.tile_cols), BF16),
        pltpu.VMEM((s.rank, s.pixels), BF16),
        pltpu.VMEM((s.rank, s.width), BF16),
        pltpu.SMEM((s.slots,), jnp.int32),
        pltpu.SMEM((s.slots,), jnp.int32),
        pltpu.SMEM((1, 1), jnp.int32),
        pltpu.VMEM((8, LANE), jnp.int32),
        pltpu.SMEM((8, LANE), jnp.int32),
        pltpu.VMEM((2, s.realiz, s.pixels), F32),
        pltpu.VMEM((3, s.pixels, s.pixels), BF16),
        pltpu.VMEM((s.nq, s.pixels, s.chunk), BF16),
        pltpu.VMEM((2, 2, s.nx, s.tb, *tile), BF16),
        pltpu.VMEM((2, 2, s.nx, s.tb, *tile), BF16),
        pltpu.VMEM((2, 2, s.nx - 1, s.tb, *tile), BF16),
        pltpu.VMEM((2, 2, s.nx - 1, s.tb, *tile), BF16),
        pltpu.VMEM((2, 2, s.tq, *tile), BF16),
        pltpu.VMEM((2, 2, s.ny - 1, s.tp, *tile), BF16),
        pltpu.VMEM((2, s.nq, 2, s.tq, *tile), BF16),
        pltpu.VMEM((2, s.fz, *tile), BF16),
        pltpu.VMEM((2, s.nz - 1, s.zp, *tile), BF16),
        pltpu.VMEM((2, s.fz, *tile), BF16),
        pltpu.VMEM((s.realiz, s.pixels), F32),
        pltpu.VMEM((2, s.realiz, LANE), F32),
        pltpu.VMEM((2, s.realiz, LANE), F32),
        pltpu.VMEM((s.realiz, LANE), F32),
        pltpu.VMEM((2, s.tp, *tile), F32),
        pltpu.VMEM((2, s.groups, *tile), F32),
        pltpu.VMEM((3, 8, LANE), F32),
        pltpu.VMEM((3, s.nq - 1, 8, LANE), F32),
        pltpu.VMEM((3, 8, LANE), F32),
        pltpu.VMEM((3, s.ny - 1, 8, LANE), F32),
        pltpu.VMEM((2, 8, LANE), F32),
        pltpu.VMEM((2, s.nz - 1, 8, LANE), F32),
        dma((9,)),
        dma((1,)),
        dma((2,)),
        dma((2, 2)),
        dma((2, 2, s.nx)),
        dma((2, 2)),
        dma((2, 2, s.nx - 1)),
        dma((2, 2)),
        dma((2, 2)),
        dma((2, 2)),
        dma((2, 2)),
        dma((2, 2)),
        dma((2, 2, s.nx - 1)),
        dma((2, 2)),
        dma((2, 2, s.nx)),
        dma((2,)),
        dma((2,)),
        dma((2,)),
        dma((2,)),
        dma((3,)),
        dma((3,)),
        dma((3,)),
        dma((3,)),
        dma((2,)),
        dma((2,)),
    ]


def far_first(count):
    return sorted(range(1, count), key=lambda d: (-min(d, count - d), d))


def near_first(count):
    return sorted(range(1, count), key=lambda d: (min(d, count - d), d))


def await_bytes(ref, sem):
    pltpu.make_async_copy(ref, ref, sem).wait()


def to_row(column):
    rows = column.shape[0]
    wide = jnp.broadcast_to(column, (rows, LANE))
    wide = jnp.concatenate([wide, jnp.zeros((LANE - rows, LANE), F32)], axis=0)
    return wide.T[0:8]


def from_row(row, rows):
    return jnp.broadcast_to(row[0:1], (LANE, LANE)).T[0:rows]


def row_sums(blocks):
    total = blocks[0] * blocks[0]
    for block in blocks[1:]:
        total = total + block * block
    return jnp.sum(total, axis=1, keepdims=True)


def lane_blocks(value):
    return [value[:, j * LANE : (j + 1) * LANE] for j in range(value.shape[1] // LANE)]


def as_tiles(value):
    groups = value.shape[0] // TILE
    return jnp.concatenate([b.reshape(groups, TILE, LANE) for b in lane_blocks(value)], axis=0)


def from_tiles(tiles, groups):
    count = tiles.shape[0] // groups
    return jnp.concatenate(
        [tiles[j * groups : (j + 1) * groups].reshape(groups * TILE, LANE) for j in range(count)], axis=1
    )


def three_parts(value):
    high = value.astype(BF16)
    rest = value - high.astype(F32)
    middle = rest.astype(BF16)
    low = (rest - middle.astype(F32)).astype(BF16)
    return jnp.concatenate([high, middle, low], axis=0)


def kernel(
    s, data_hbm, source_hbm, rows_hbm, cols_hbm, count_hbm, tiles_hbm, left_hbm, right_hbm, slip, misfit,
    data, source, tiles, far_left, far_right, near_rows, near_cols, near_count, table, table_s, halo, onehot, g,
    pc_send, pc_recv, px_send, px_recv, q_send, q_recv, v, f_send, f_recv, f_all, left, alphas, betas, inverse,
    previous, coef, sa_send, sa_recv, sb_send, sb_recv, sz_send, sz_recv, in_sem, halo_ss, halo_rs, c_ss, c_rs,
    x_ss, x_rs, y_ss, y_rs, yg_ss, yg_rs, xg_ss, xg_rs, cg_ss, cg_rs, z_ss, z_rs, zg_ss, zg_rs, sa_ss, sa_rs,
    sb_ss, sb_rs, sz_ss, sz_rs,
):
    place = lax.axis_index("rows")
    z = lax.axis_index("cols")
    core = lax.rem(place, 2)
    chip = place // 2
    y = lax.rem(chip, s.ny)
    x = chip // s.ny
    other = 1 - core
    own_q = core * s.nx + x
    n = s.realiz

    def at(xx, yy, cc):
        return ((xx * s.ny + yy) * 2 + cc, z)

    def cross(d):
        q = lax.rem(own_q + d, s.nq)
        return at(lax.rem(q, s.nx), y, q // s.nx)

    def beside(d):
        return lax.rem(x + d + s.nx, s.nx)

    mate = at(x, y, other)
    crosses = [None] + [cross(d) for d in range(1, s.nq)]
    in_x = [None] + [at(beside(d), y, core) for d in range(1, s.nx)]
    y_of = [lax.rem(y + d, s.ny) for d in range(s.ny)]
    in_y = [None] + [at(x, y_of[d], core) for d in range(1, s.ny)]
    z_of = [lax.rem(z + d, s.nz) for d in range(s.nz)]
    in_z = [None] + [(place, z_of[d]) for d in range(1, s.nz)]
    to_q = [[cc * s.nx + beside(d) for d in range(s.nx)] for cc in (core, other)]
    from_q = [[cc * s.nx + beside(-d) for d in range(s.nx)] for cc in (core, other)]

    def send(src, dst, send_sem, recv_sem, device):
        pltpu.make_async_remote_copy(
            src_ref=src, dst_ref=dst, send_sem=send_sem, recv_sem=recv_sem, device_id=device, device_id_type=MESH
        ).start()

    pairs = [
        (rows_hbm, near_rows),
        (cols_hbm, near_cols),
        (count_hbm, near_count),
        (source_hbm, source),
        (data_hbm, data),
        (left_hbm, far_left),
        (right_hbm, far_right),
        (tiles_hbm, tiles),
    ]
    loads = [pltpu.make_async_copy(src, dst, in_sem.at[k]) for k, (src, dst) in enumerate(pairs)]
    for load in loads:
        load.start()

    step_out = lax.rem(place + s.rows + 2 * core - 1, s.rows)
    partners = crosses[1:] + in_y[1:] + in_z[1:]
    partners += [(step_out, z)]
    barrier = pltpu.get_barrier_semaphore()
    for device in partners:
        pl.semaphore_signal(barrier, inc=1, device_id=device, device_id_type=MESH)

    for load in loads[:3]:
        load.wait()
    per_row = s.width // s.tile_cols
    spot = lax.broadcasted_iota(jnp.int32, (8, LANE), 1)
    slot_of = jnp.full((8, LANE), -1, jnp.int32)
    for k in range(s.slots):
        where = jnp.where(k < near_count[0, 0], near_rows[k] * per_row + near_cols[k], -1)
        slot_of = jnp.where(spot == where, k, slot_of)
    table[...] = slot_of
    to_scalars = pltpu.make_async_copy(table, table_s, in_sem.at[8])
    to_scalars.start()

    pl.semaphore_wait(barrier, len(partners))

    after = lax.rem(place + 1, s.rows)
    before = lax.rem(place + s.rows - 1, s.rows)
    loads[4].wait()
    send(data, halo.at[0], halo_ss.at[0], halo_rs.at[0], (after, z))
    send(data, halo.at[1], halo_ss.at[0], halo_rs.at[1], (before, z))

    loads[3].wait()
    total = s.rows * s.pixels
    offset = source[...] + s.pixels - place * s.pixels
    offset = jnp.where(offset < 0, offset + total, offset)
    offset = jnp.where(offset >= total, offset - total, offset)
    index = lax.broadcasted_iota(jnp.int32, (s.pixels, s.pixels), 0)
    for k in range(3):
        onehot[k] = jnp.where(index == offset - k * s.pixels, 1.0, 0.0).astype(BF16)

    for load in loads[5:]:
        load.wait()
    to_scalars.wait()
    half = per_row // 2
    half_blocks = half * s.tile_cols // LANE
    bands = s.pixels // s.tile_rows

    def build(i, carry):
        side, a = i // bands, lax.rem(i, bands)
        pixel = pl.ds(pl.multiple_of(a * s.tile_rows, s.tile_rows), s.tile_rows)
        lefts = far_left[:, pixel]
        for b in range(half):
            column = pl.ds(pl.multiple_of((side * half + b) * s.tile_cols, s.tile_cols), s.tile_cols)
            block = lax.dot_general(lefts, far_right[:, column], (((0,), (0,)), ((), ())), preferred_element_type=F32)
            slot = table_s[0, a * per_row + side * half + b]
            near = tiles[jnp.maximum(slot, 0)].astype(F32)
            block = (block + near * jnp.where(slot >= 0, 1.0, 0.0)).astype(BF16)
            for k in range(s.tile_cols // LANE):
                j = b * (s.tile_cols // LANE) + k
                q = side * (half_blocks // s.nb) + j // s.nb
                lane = (j % s.nb) * LANE
                g[q, pixel, lane : lane + LANE] = block[:, k * LANE : (k + 1) * LANE]
        return carry

    lax.fori_loop(0, 2 * bands, build, 0)

    seen = jnp.dot(three_parts(data[...]), onehot[1], preferred_element_type=F32)
    for k in range(2):
        await_bytes(halo.at[k], halo_rs.at[k])
        seen = seen + jnp.dot(three_parts(halo[k]), onehot[2 * k], preferred_element_type=F32)
    observed = (seen[0:n] + seen[n : 2 * n]) + seen[2 * n : 3 * n]
    misfit[...] = observed
    left[...] = observed
    previous[...] = jnp.zeros_like(previous)
    inverse[...] = jnp.zeros_like(inverse)

    def sum_start(i, column):
        sa_send[i] = to_row(column)
        for d in range(1, s.nq):
            send(sa_send.at[i], sa_recv.at[i, d - 1], sa_ss.at[i], sa_rs.at[i], crosses[d])

    def sum_middle(i):
        await_bytes(sa_recv.at[i], sa_rs.at[i])
        sb_send[i] = sa_send[i] + jnp.sum(sa_recv[i], axis=0)
        for d in range(1, s.ny):
            send(sb_send.at[i], sb_recv.at[i, d - 1], sb_ss.at[i], sb_rs.at[i], in_y[d])

    def sum_end(i):
        await_bytes(sb_recv.at[i], sb_rs.at[i])
        return jnp.sqrt(from_row(sb_send[i] + jnp.sum(sb_recv[i], axis=0), n) + EPSILON)

    def square_sums(it):
        def squares(q, running):
            for p, part in enumerate(s.parts):
                for j in range(part.blocks):
                    block = v[it, q, p, j * s.groups : (j + 1) * s.groups].astype(F32).reshape(n, LANE)
                    running = running + block * block
            return running

        running = lax.fori_loop(0, s.nq, squares, jnp.zeros((n, LANE), F32))
        return jnp.sum(running, axis=1, keepdims=True)

    def predicted(it, j):
        return f_all[it, j * s.groups : (j + 1) * s.groups].astype(F32).reshape(n, LANE)

    def left_sums():
        return row_sums(lane_blocks(left[...]))

    def iteration(it, carry):
        pixel_b = left[...].astype(BF16)

        def product(p, q):
            return as_tiles(jnp.dot(pixel_b, g[q, :, s.parts[p].lanes], preferred_element_type=F32))

        def to_mate(p, d):
            tb = s.parts[p].tb
            mine = pc_send.at[it, p, d, 0:tb]
            mine[...] = product(p, to_q[1][d]).astype(BF16)
            send(mine, pc_recv.at[it, p, d, 0:tb], c_ss.at[it, p], c_rs.at[it, p, d], mate)

        def pair_sum(p, d):
            own = product(p, to_q[0][d])
            came = pc_recv.at[it, p, d, 0 : s.parts[p].tb]
            await_bytes(came, c_rs.at[it, p, d])
            return own + came[...].astype(F32)

        def scatter_x(p, d):
            mine = px_send.at[it, p, d - 1, 0 : s.parts[p].tb]
            mine[...] = pair_sum(p, d).astype(BF16)
            send(mine, px_recv.at[it, p, d - 1, 0 : s.parts[p].tb], x_ss.at[it, p], x_rs.at[it, p, d - 1], in_x[d])

        def scatter_y(p):
            tb, tp, tq = s.parts[p].tb, s.parts[p].tp, s.parts[p].tq
            own = pair_sum(p, 0)
            for d in near_first(s.nx):
                came = px_recv.at[it, p, d - 1, 0:tb]
                await_bytes(came, x_rs.at[it, p, d - 1])
                own = own + came[...].astype(F32)
            q_send[it, p, 0:tb] = own.astype(BF16)
            if tq > tb:
                q_send[it, p, tb:tq] = jnp.zeros((tq - tb, TILE, LANE), BF16)
            for d in far_first(s.ny):
                piece = q_send.at[it, p, pl.ds(y_of[d] * tp, tp)]
                send(piece, q_recv.at[it, p, d - 1, 0:tp], y_ss.at[it, p], y_rs.at[it, p], in_y[d])

        def spread_y(p):
            tp = s.parts[p].tp
            await_bytes(q_recv.at[it, p, :, 0:tp], y_rs.at[it, p])
            share = q_send[it, p, pl.ds(y * tp, tp)].astype(F32)
            for d in range(s.ny - 1):
                share = share + q_recv[it, p, d, 0:tp].astype(F32)
            mine = v.at[it, own_q, p, pl.ds(y * tp, tp)]
            for i in range(tp):
                group = lax.rem(y * tp + i, s.groups)
                raw = share[i] * coef[0, group] - previous[p, i] * coef[1, group]
                previous[p, i] = raw
                v[it, own_q, p, y * tp + i] = raw.astype(BF16)
            for d in far_first(s.ny):
                send(mine, mine, yg_ss.at[it, p], yg_rs.at[it, p], in_y[d])

        def applied(p, q):
            return lax.dot_general(
                from_tiles(v[it, q, p, 0 : s.parts[p].tb], s.groups),
                g[q, :, s.parts[p].lanes],
                (((1,), (1,)), ((), ())),
                preferred_element_type=F32,
            )

        order = far_first(s.nx)
        for d in order:
            to_mate(0, d)
        for d in order:
            scatter_x(0, d)
        sum_start(it, left_sums())
        to_mate(0, 0)
        for d in order:
            to_mate(1, d)
        for d in order:
            scatter_x(1, d)
        sum_middle(it)
        scatter_y(0)
        to_mate(1, 0)
        scatter_y(1)
        beta = sum_end(it)
        betas[it] = beta
        coef[0] = (1.0 / beta).reshape(s.groups, TILE, LANE)
        coef[1] = (beta * inverse[...]).reshape(s.groups, TILE, LANE)
        for p in range(2):
            spread_y(p)

        total = jnp.zeros((n, s.pixels), F32)
        for p, part in enumerate(s.parts):
            await_bytes(q_recv.at[it, p, :, 0 : part.tp], yg_rs.at[it, p])
            ready = v.at[it, own_q, p, 0 : part.tb]
            for d in far_first(s.nx):
                send(ready, ready, xg_ss.at[it, p], xg_rs.at[it, p, d - 1], in_x[d])
            send(ready, ready, cg_ss.at[it, p], cg_rs.at[it, p, 0], mate)
            total = total + applied(p, own_q)
        for p, part in enumerate(s.parts):
            for d in near_first(s.nx):
                q = from_q[0][d]
                came = v.at[it, q, p, 0 : part.tb]
                await_bytes(came, xg_rs.at[it, p, d - 1])
                send(came, came, cg_ss.at[it, p], cg_rs.at[it, p, d], mate)
                total = total + applied(p, q)
            for d in [0] + near_first(s.nx):
                q = from_q[1][d]
                await_bytes(v.at[it, q, p, 0 : part.tb], cg_rs.at[it, p, d])
                total = total + applied(p, q)

        f_send[it, 0 : s.ft] = as_tiles(total).astype(BF16)
        if s.fz > s.ft:
            f_send[it, s.ft : s.fz] = jnp.zeros((s.fz - s.ft, TILE, LANE), BF16)
        for d in far_first(s.nz):
            piece = f_send.at[it, pl.ds(z_of[d] * s.zp, s.zp)]
            send(piece, f_recv.at[it, d - 1], z_ss.at[it], z_rs.at[it], in_z[d])
        sz_send[it] = to_row(square_sums(it))
        for d in far_first(s.nz):
            send(sz_send.at[it], sz_recv.at[it, d - 1], sz_ss.at[it], sz_rs.at[it], in_z[d])
        await_bytes(f_recv.at[it], z_rs.at[it])
        reduced = f_send[it, pl.ds(z * s.zp, s.zp)].astype(F32)
        for d in range(s.nz - 1):
            reduced = reduced + f_recv[it, d].astype(F32)
        mine = f_all.at[it, pl.ds(z * s.zp, s.zp)]
        mine[...] = reduced.astype(BF16)
        for d in far_first(s.nz):
            send(mine, mine, zg_ss.at[it], zg_rs.at[it], in_z[d])
        await_bytes(sz_recv.at[it], sz_rs.at[it])
        alpha = jnp.sqrt(from_row(sz_send[it] + jnp.sum(sz_recv[it], axis=0), n) + EPSILON)
        alphas[it] = alpha
        inverse[...] = 1.0 / alpha
        ratio = alpha / beta
        await_bytes(f_recv.at[it], zg_rs.at[it])
        for j in range(s.fb):
            lanes = slice(j * LANE, (j + 1) * LANE)
            left[:, lanes] = predicted(it, j) * inverse[...] - left[:, lanes] * ratio
        return carry

    lax.fori_loop(0, 2, iteration, 0)

    sum_start(2, left_sums())
    alpha1, alpha2, beta1, beta2 = alphas[0], alphas[1], betas[0], betas[1]
    rho1 = jnp.sqrt(alpha1 * alpha1 + beta2 * beta2)
    cosine, sine = alpha1 / rho1, beta2 / rho1
    phi1 = cosine * beta1
    phibar = sine * beta1
    theta = sine * alpha2
    rhobar = -cosine * alpha2

    first = place * (s.width // s.rows)
    block = first // LANE
    lane = lax.rem(first, LANE)
    share_width = s.width // s.rows
    cover = -(-share_width // LANE)
    shape = ((cover + 1) * LANE, cover * LANE)
    pick = lax.broadcasted_iota(jnp.int32, shape, 0) == lax.broadcasted_iota(jnp.int32, shape, 1) + lane
    pick = jnp.where(pick, 1.0, 0.0).astype(BF16)
    window = []
    for it in range(2):
        sides = []
        for k in range(cover + 1):
            b = jnp.minimum(block + k, s.width // LANE - 1)
            j = lax.rem(b, s.nb)
            p = j // s.cut
            inside = (j - p * s.cut) * s.groups
            sides.append(v[it, b // s.nb, p, pl.ds(inside, s.groups)].reshape(n, LANE))
        window.append(jnp.dot(jnp.concatenate(sides, axis=1), pick, preferred_element_type=F32))

    sum_middle(2)
    beta3 = sum_end(2)
    rho2 = jnp.sqrt(rhobar * rhobar + beta3 * beta3)
    phi2 = rhobar / rho2 * phibar
    on2 = phi2 / rho2
    weight1 = (phi1 / rho1 - on2 * (theta / rho1)) / alpha1
    weight2 = on2 / alpha2
    result = [weight1 * a + weight2 * b for a, b in zip(lane_blocks(window[0]), lane_blocks(window[1]), strict=True)]
    slip[...] = jnp.concatenate(result, axis=1)[:, 0:share_width]
    for j in range(s.fb):
        lanes = slice(j * LANE, (j + 1) * LANE)
        misfit[:, lanes] = misfit[:, lanes] - weight1 * predicted(0, j) - weight2 * predicted(1, j)

    await_bytes(halo, halo_ss.at[0])

    def settle(it, carry):
        for p, part in enumerate(s.parts):
            four = pc_send.at[it, p, :, 0 : part.tb]
            three = px_send.at[it, p, :, 0 : part.tb]
            pieces = q_recv.at[it, p, :, 0 : part.tp]
            await_bytes(four, c_ss.at[it, p])
            await_bytes(three, x_ss.at[it, p])
            await_bytes(pieces, y_ss.at[it, p])
            await_bytes(pieces, yg_ss.at[it, p])
            await_bytes(three, xg_ss.at[it, p])
            await_bytes(four, cg_ss.at[it, p])
        await_bytes(f_recv.at[it], z_ss.at[it])
        await_bytes(f_recv.at[it], zg_ss.at[it])
        await_bytes(sz_recv.at[it], sz_ss.at[it])
        return carry

    lax.fori_loop(0, 2, settle, 0)
    for i in range(3):
        await_bytes(sa_recv.at[i], sa_ss.at[i])
        await_bytes(sb_recv.at[i], sb_ss.at[i])


def body(dims, nz, data, source, near_tiles, near_rows, near_cols, near_count, far_left, far_right):
    realiz, pixels = data.shape
    rank, width = far_right.shape
    slots, tile_rows, tile_cols = near_tiles.shape
    s = Sizes(dims, nz, realiz, pixels, width, slots, rank, tile_rows, tile_cols)
    vmem = pl.BlockSpec(memory_space=pltpu.VMEM)
    pin = functools.partial(pltpu.with_memory_space_constraint, memory_space=pltpu.HBM)
    return pl.pallas_call(
        functools.partial(kernel, s),
        out_shape=(pltpu.VMEM((realiz, width // s.rows), F32), pltpu.VMEM((realiz, pixels), F32)),
        in_specs=[pl.BlockSpec(memory_space=pl.ANY)] * 8,
        out_specs=(vmem, vmem),
        scratch_shapes=scratch_shapes(s),
        compiler_params=pltpu.CompilerParams(
            collective_id=0, has_side_effects=True, vmem_limit_bytes=48 * 1024 * 1024
        ),
    )(
        pin(data),
        pin(source.reshape(1, pixels)),
        pin(near_rows.reshape(slots)),
        pin(near_cols.reshape(slots)),
        near_count,
        pin(near_tiles),
        pin(far_left),
        pin(far_right),
    )


def solution(mesh, dims=(4, 8, 2)):
    return jax.shard_map(
        functools.partial(body, dims, mesh.shape["cols"]),
        mesh=mesh,
        in_specs=(
            P(None, "rows"),
            P("rows"),
            P("rows", "cols", None),
            P("rows", "cols"),
            P("rows", "cols"),
            P("rows", "cols"),
            P("cols", "rows"),
            P("rows", "cols"),
        ),
        out_specs=(P(None, ("cols", "rows")), P(None, "rows")),
        check_vma=False,
    )
```

```python
import functools

import jax
import jax.numpy as jnp
from jax import lax
from jax.experimental import pallas as pl
from jax.experimental.pallas import tpu as pltpu
from jax.sharding import PartitionSpec as P

EPSILON = 1e-06
LANE = 128
TILE = 16
MESH = pl.DeviceIdType.MESH
F32 = jnp.float32
BF16 = jnp.bfloat16


class Part:
    def __init__(self, first, blocks, s):
        self.lanes = slice(first * LANE, (first + blocks) * LANE)
        self.blocks = blocks
        self.tb = blocks * s.groups
        self.tp = -(-self.tb // s.ny)
        self.tq = self.tp * s.ny
        half = (self.tb + 1) // 2
        self.halves = ((0, half), (half, self.tb))


class Sizes:
    def __init__(self, dims, nz, realiz, pixels, width, slots, rank, tile_rows, tile_cols):
        self.nx, self.ny, self.cores = dims
        self.nz = nz
        self.rows = self.nx * self.ny * self.cores
        self.nq = self.nx * self.cores
        self.realiz, self.pixels, self.width = realiz, pixels, width
        self.slots, self.rank, self.tile_rows, self.tile_cols = slots, rank, tile_rows, tile_cols
        self.groups = realiz // TILE
        self.chunk = width // self.nq
        self.nb = self.chunk // LANE
        self.fb = pixels // LANE
        self.ft = self.fb * self.groups
        self.zp = -(-self.ft // nz)
        self.fz = self.zp * nz
        self.cut = (self.nb + 1) // 2
        self.parts = [Part(0, self.cut, self), Part(self.cut, self.nb - self.cut, self)]
        self.tb = max(p.tb for p in self.parts)
        self.tp = max(p.tp for p in self.parts)
        self.tq = max(p.tq for p in self.parts)


def scratch_shapes(s):
    dma = pltpu.SemaphoreType.DMA
    tile = (TILE, LANE)
    return [
        pltpu.VMEM((s.realiz, s.pixels), F32),
        pltpu.VMEM((1, s.pixels), jnp.int32),
        pltpu.VMEM((s.slots + 1, s.tile_rows, s.tile_cols), BF16),
        pltpu.VMEM((s.rank, s.pixels), BF16),
        pltpu.VMEM((s.rank, s.width), BF16),
        pltpu.SMEM((s.slots,), jnp.int32),
        pltpu.SMEM((s.slots,), jnp.int32),
        pltpu.SMEM((1, 1), jnp.int32),
        pltpu.VMEM((8, LANE), jnp.int32),
        pltpu.SMEM((8, LANE), jnp.int32),
        pltpu.VMEM((2, s.realiz, s.pixels), F32),
        pltpu.VMEM((3, s.pixels, s.pixels), BF16),
        pltpu.VMEM((s.nq, s.pixels, s.chunk), BF16),
        pltpu.VMEM((2, 2, s.nx, s.tb, *tile), BF16),
        pltpu.VMEM((2, 2, s.nx, s.tb, *tile), BF16),
        pltpu.VMEM((2, 2, s.nx - 1, s.tb, *tile), BF16),
        pltpu.VMEM((2, 2, s.nx - 1, s.tb, *tile), BF16),
        pltpu.VMEM((2, 2, s.tq, *tile), BF16),
        pltpu.VMEM((2, 2, s.ny - 1, s.tp, *tile), BF16),
        pltpu.VMEM((2, s.nq, 2, s.tq, *tile), BF16),
        pltpu.VMEM((2, s.fz, *tile), BF16),
        pltpu.VMEM((2, s.nz - 1, s.zp, *tile), BF16),
        pltpu.VMEM((2, s.fz, *tile), BF16),
        pltpu.VMEM((s.realiz, s.pixels), F32),
        pltpu.VMEM((2, s.realiz, LANE), F32),
        pltpu.VMEM((2, s.realiz, LANE), F32),
        pltpu.VMEM((s.realiz, LANE), F32),
        pltpu.VMEM((2, s.tp, *tile), F32),
        pltpu.VMEM((2, s.groups, *tile), F32),
        pltpu.VMEM((3, 8, LANE), F32),
        pltpu.VMEM((3, s.nq - 1, 8, LANE), F32),
        pltpu.VMEM((3, 8, LANE), F32),
        pltpu.VMEM((3, s.ny - 1, 8, LANE), F32),
        pltpu.VMEM((2, 8, LANE), F32),
        pltpu.VMEM((2, s.nz - 1, 8, LANE), F32),
        dma((9,)),
        dma((1,)),
        dma((2,)),
        dma((2, 2)),
        dma((2, 2, s.nx)),
        dma((2, 2)),
        dma((2, 2, s.nx - 1)),
        dma((2, 2)),
        dma((2, 2)),
        dma((2, 2)),
        dma((2, 2)),
        dma((2, 2)),
        dma((2, 2, 4)),
        dma((2, 2)),
        dma((2, 2, 5)),
        dma((2,)),
        dma((2,)),
        dma((2,)),
        dma((2,)),
        dma((3,)),
        dma((3,)),
        dma((3,)),
        dma((3,)),
        dma((2,)),
        dma((2,)),
    ]


def far_first(count):
    return sorted(range(1, count), key=lambda d: (-min(d, count - d), d))


def near_first(count):
    return sorted(range(1, count), key=lambda d: (min(d, count - d), d))


def await_bytes(ref, sem):
    pltpu.make_async_copy(ref, ref, sem).wait()


def to_row(column):
    rows = column.shape[0]
    wide = jnp.broadcast_to(column, (rows, LANE))
    wide = jnp.concatenate([wide, jnp.zeros((LANE - rows, LANE), F32)], axis=0)
    return wide.T[0:8]


def from_row(row, rows):
    return jnp.broadcast_to(row[0:1], (LANE, LANE)).T[0:rows]


def row_sums(blocks):
    total = blocks[0] * blocks[0]
    for block in blocks[1:]:
        total = total + block * block
    return jnp.sum(total, axis=1, keepdims=True)


def lane_blocks(value):
    return [value[:, j * LANE : (j + 1) * LANE] for j in range(value.shape[1] // LANE)]


def as_tiles(value):
    groups = value.shape[0] // TILE
    return jnp.concatenate([b.reshape(groups, TILE, LANE) for b in lane_blocks(value)], axis=0)


def from_tiles(tiles, groups):
    count = tiles.shape[0] // groups
    return jnp.concatenate(
        [tiles[j * groups : (j + 1) * groups].reshape(groups * TILE, LANE) for j in range(count)], axis=1
    )


def three_parts(value):
    high = value.astype(BF16)
    rest = value - high.astype(F32)
    middle = rest.astype(BF16)
    low = (rest - middle.astype(F32)).astype(BF16)
    return jnp.concatenate([high, middle, low], axis=0)


def kernel(
    s, data_hbm, source_hbm, rows_hbm, cols_hbm, count_hbm, tiles_hbm, left_hbm, right_hbm, slip, misfit,
    data, source, tiles, far_left, far_right, near_rows, near_cols, near_count, table, table_s, halo, onehot, g,
    pc_send, pc_recv, px_send, px_recv, q_send, q_recv, v, f_send, f_recv, f_all, left, alphas, betas, inverse,
    previous, coef, sa_send, sa_recv, sb_send, sb_recv, sz_send, sz_recv, in_sem, halo_ss, halo_rs, c_ss, c_rs,
    x_ss, x_rs, y_ss, y_rs, yg_ss, yg_rs, xg_ss, xg_rs, cg_ss, cg_rs, z_ss, z_rs, zg_ss, zg_rs, sa_ss, sa_rs,
    sb_ss, sb_rs, sz_ss, sz_rs,
):
    place = lax.axis_index("rows")
    z = lax.axis_index("cols")
    core = lax.rem(place, 2)
    chip = place // 2
    y = lax.rem(chip, s.ny)
    x = chip // s.ny
    other = 1 - core
    own_q = core * s.nx + x
    n = s.realiz

    def at(xx, yy, cc):
        return ((xx * s.ny + yy) * 2 + cc, z)

    def cross(d):
        q = lax.rem(own_q + d, s.nq)
        return at(lax.rem(q, s.nx), y, q // s.nx)

    def beside(d):
        return lax.rem(x + d + s.nx, s.nx)

    mate = at(x, y, other)
    crosses = [None] + [cross(d) for d in range(1, s.nq)]
    in_x = [None] + [at(beside(d), y, core) for d in range(1, s.nx)]
    y_of = [lax.rem(y + d, s.ny) for d in range(s.ny)]
    in_y = [None] + [at(x, y_of[d], core) for d in range(1, s.ny)]
    z_of = [lax.rem(z + d, s.nz) for d in range(s.nz)]
    in_z = [None] + [(place, z_of[d]) for d in range(1, s.nz)]
    to_q = [[cc * s.nx + beside(d) for d in range(s.nx)] for cc in (core, other)]
    from_q = [[cc * s.nx + beside(-d) for d in range(s.nx)] for cc in (core, other)]

    def send(src, dst, send_sem, recv_sem, device):
        pltpu.make_async_remote_copy(
            src_ref=src, dst_ref=dst, send_sem=send_sem, recv_sem=recv_sem, device_id=device, device_id_type=MESH
        ).start()

    pairs = [
        (rows_hbm, near_rows),
        (cols_hbm, near_cols),
        (count_hbm, near_count),
        (source_hbm, source),
        (data_hbm, data),
        (left_hbm, far_left),
        (right_hbm, far_right),
        (tiles_hbm, tiles.at[0 : s.slots]),
    ]
    loads = [pltpu.make_async_copy(src, dst, in_sem.at[k]) for k, (src, dst) in enumerate(pairs)]
    for load in loads:
        load.start()

    step_out = lax.rem(place + s.rows + 2 * core - 1, s.rows)
    partners = crosses[1:] + in_y[1:] + in_z[1:]
    partners += [(step_out, z)]
    barrier = pltpu.get_barrier_semaphore()
    for device in partners:
        pl.semaphore_signal(barrier, inc=1, device_id=device, device_id_type=MESH)

    tiles[s.slots] = jnp.zeros((s.tile_rows, s.tile_cols), BF16)
    for load in loads[:3]:
        load.wait()
    per_row = s.width // s.tile_cols
    spot = lax.broadcasted_iota(jnp.int32, (8, LANE), 1)
    slot_of = jnp.full((8, LANE), s.slots, jnp.int32)
    for k in range(s.slots):
        where = jnp.where(k < near_count[0, 0], near_rows[k] * per_row + near_cols[k], -1)
        slot_of = jnp.where(spot == where, k, slot_of)
    table[...] = slot_of
    to_scalars = pltpu.make_async_copy(table, table_s, in_sem.at[8])
    to_scalars.start()

    pl.semaphore_wait(barrier, len(partners))

    after = lax.rem(place + 1, s.rows)
    before = lax.rem(place + s.rows - 1, s.rows)
    loads[4].wait()
    send(data, halo.at[0], halo_ss.at[0], halo_rs.at[0], (after, z))
    send(data, halo.at[1], halo_ss.at[0], halo_rs.at[1], (before, z))

    loads[3].wait()
    total = s.rows * s.pixels
    offset = source[...] + s.pixels - place * s.pixels
    offset = jnp.where(offset < 0, offset + total, offset)
    offset = jnp.where(offset >= total, offset - total, offset)
    index = lax.broadcasted_iota(jnp.int32, (s.pixels, s.pixels), 0)
    for k in range(3):
        onehot[k] = jnp.where(index == offset - k * s.pixels, 1.0, 0.0).astype(BF16)

    for load in loads[5:]:
        load.wait()
    to_scalars.wait()
    half = per_row // 2
    half_blocks = half * s.tile_cols // LANE
    bands = s.pixels // s.tile_rows

    def build(i, carry):
        side, a = i // bands, lax.rem(i, bands)
        pixel = pl.ds(pl.multiple_of(a * s.tile_rows, s.tile_rows), s.tile_rows)
        lefts = far_left[:, pixel]
        for b in range(half):
            column = pl.ds(pl.multiple_of((side * half + b) * s.tile_cols, s.tile_cols), s.tile_cols)
            block = lax.dot_general(lefts, far_right[:, column], (((0,), (0,)), ((), ())), preferred_element_type=F32)
            near = tiles[table_s[0, a * per_row + side * half + b]]
            block = (block + near.astype(F32)).astype(BF16)
            for k in range(s.tile_cols // LANE):
                j = b * (s.tile_cols // LANE) + k
                q = side * (half_blocks // s.nb) + j // s.nb
                lane = (j % s.nb) * LANE
                g[q, pixel, lane : lane + LANE] = block[:, k * LANE : (k + 1) * LANE]
        return carry

    lax.fori_loop(0, 2 * bands, build, 0)

    seen = jnp.dot(three_parts(data[...]), onehot[1], preferred_element_type=F32)
    for k in range(2):
        await_bytes(halo.at[k], halo_rs.at[k])
        seen = seen + jnp.dot(three_parts(halo[k]), onehot[2 * k], preferred_element_type=F32)
    observed = (seen[0:n] + seen[n : 2 * n]) + seen[2 * n : 3 * n]
    misfit[...] = observed
    left[...] = observed
    previous[...] = jnp.zeros_like(previous)
    inverse[...] = jnp.zeros_like(inverse)

    def sum_start(i, column):
        sa_send[i] = to_row(column)
        for d in range(1, s.nq):
            send(sa_send.at[i], sa_recv.at[i, d - 1], sa_ss.at[i], sa_rs.at[i], crosses[d])

    def sum_middle(i):
        await_bytes(sa_recv.at[i], sa_rs.at[i])
        sb_send[i] = sa_send[i] + jnp.sum(sa_recv[i], axis=0)
        for d in range(1, s.ny):
            send(sb_send.at[i], sb_recv.at[i, d - 1], sb_ss.at[i], sb_rs.at[i], in_y[d])

    def sum_end(i):
        await_bytes(sb_recv.at[i], sb_rs.at[i])
        return jnp.sqrt(from_row(sb_send[i] + jnp.sum(sb_recv[i], axis=0), n) + EPSILON)

    def square_sums(it):
        def squares(q, running):
            for p, part in enumerate(s.parts):
                for j in range(part.blocks):
                    block = v[it, q, p, j * s.groups : (j + 1) * s.groups].astype(F32).reshape(n, LANE)
                    running = running + block * block
            return running

        running = lax.fori_loop(0, s.nq, squares, jnp.zeros((n, LANE), F32))
        return jnp.sum(running, axis=1, keepdims=True)

    def predicted(it, j):
        return f_all[it, j * s.groups : (j + 1) * s.groups].astype(F32).reshape(n, LANE)

    def left_sums():
        return row_sums(lane_blocks(left[...]))

    def iteration(it, carry):
        pixel_b = left[...].astype(BF16)

        def product(p, q):
            return as_tiles(jnp.dot(pixel_b, g[q, :, s.parts[p].lanes], preferred_element_type=F32))

        def to_mate(p, d):
            tb = s.parts[p].tb
            mine = pc_send.at[it, p, d, 0:tb]
            mine[...] = product(p, to_q[1][d]).astype(BF16)
            send(mine, pc_recv.at[it, p, d, 0:tb], c_ss.at[it, p], c_rs.at[it, p, d], mate)

        def pair_sum(p, d):
            own = product(p, to_q[0][d])
            came = pc_recv.at[it, p, d, 0 : s.parts[p].tb]
            await_bytes(came, c_rs.at[it, p, d])
            return own + came[...].astype(F32)

        def scatter_x(p, d):
            mine = px_send.at[it, p, d - 1, 0 : s.parts[p].tb]
            mine[...] = pair_sum(p, d).astype(BF16)
            send(mine, px_recv.at[it, p, d - 1, 0 : s.parts[p].tb], x_ss.at[it, p], x_rs.at[it, p, d - 1], in_x[d])

        def scatter_y(p):
            tb, tp, tq = s.parts[p].tb, s.parts[p].tp, s.parts[p].tq
            own = pair_sum(p, 0)
            for d in near_first(s.nx):
                came = px_recv.at[it, p, d - 1, 0:tb]
                await_bytes(came, x_rs.at[it, p, d - 1])
                own = own + came[...].astype(F32)
            q_send[it, p, 0:tb] = own.astype(BF16)
            if tq > tb:
                q_send[it, p, tb:tq] = jnp.zeros((tq - tb, TILE, LANE), BF16)
            for d in far_first(s.ny):
                piece = q_send.at[it, p, pl.ds(y_of[d] * tp, tp)]
                send(piece, q_recv.at[it, p, d - 1, 0:tp], y_ss.at[it, p], y_rs.at[it, p], in_y[d])

        def spread_y(p):
            tp = s.parts[p].tp
            await_bytes(q_recv.at[it, p, :, 0:tp], y_rs.at[it, p])
            share = q_send[it, p, pl.ds(y * tp, tp)].astype(F32)
            for d in range(s.ny - 1):
                share = share + q_recv[it, p, d, 0:tp].astype(F32)
            mine = v.at[it, own_q, p, pl.ds(y * tp, tp)]
            for i in range(tp):
                group = lax.rem(y * tp + i, s.groups)
                raw = share[i] * coef[0, group] - previous[p, i] * coef[1, group]
                previous[p, i] = raw
                v[it, own_q, p, y * tp + i] = raw.astype(BF16)
            for d in far_first(s.ny):
                send(mine, mine, yg_ss.at[it, p], yg_rs.at[it, p], in_y[d])

        def applied(p, q):
            return lax.dot_general(
                from_tiles(v[it, q, p, 0 : s.parts[p].tb], s.groups),
                g[q, :, s.parts[p].lanes],
                (((1,), (1,)), ((), ())),
                preferred_element_type=F32,
            )

        order = far_first(s.nx)
        for d in order:
            to_mate(0, d)
        for d in order:
            scatter_x(0, d)
        sum_start(it, left_sums())
        to_mate(0, 0)
        for d in order:
            to_mate(1, d)
        for d in order:
            scatter_x(1, d)
        sum_middle(it)
        scatter_y(0)
        to_mate(1, 0)
        scatter_y(1)
        beta = sum_end(it)
        betas[it] = beta
        coef[0] = (1.0 / beta).reshape(s.groups, TILE, LANE)
        coef[1] = (beta * inverse[...]).reshape(s.groups, TILE, LANE)
        for p in range(2):
            spread_y(p)

        total = jnp.zeros((n, s.pixels), F32)
        for p, part in enumerate(s.parts):
            await_bytes(q_recv.at[it, p, :, 0 : part.tp], yg_rs.at[it, p])
            ready = v.at[it, own_q, p, 0 : part.tb]
            for k, device in enumerate((in_x[1], in_x[-1])):
                send(ready, ready, xg_ss.at[it, p], xg_rs.at[it, p, k], device)
            send(ready, ready, cg_ss.at[it, p], cg_rs.at[it, p, 0], mate)
            total = total + applied(p, own_q)
        for p, part in enumerate(s.parts):
            for k, d in enumerate((1, -1)):
                q = from_q[0][d]
                came = v.at[it, q, p, 0 : part.tb]
                await_bytes(came, xg_rs.at[it, p, k])
                lo, hi = part.halves[k]
                onward = v.at[it, q, p, lo:hi]
                send(onward, onward, xg_ss.at[it, p], xg_rs.at[it, p, 2 + k], in_x[d])
                send(came, came, cg_ss.at[it, p], cg_rs.at[it, p, 1 + k], mate)
            total = total + applied(p, from_q[0][1])
            total = total + applied(p, from_q[0][-1])
        for p, part in enumerate(s.parts):
            q = from_q[0][2]
            for k, (lo, hi) in enumerate(part.halves):
                came = v.at[it, q, p, lo:hi]
                await_bytes(came, xg_rs.at[it, p, 2 + k])
                send(came, came, cg_ss.at[it, p], cg_rs.at[it, p, 3 + k], mate)
            total = total + applied(p, q)
            for k, d in enumerate((0, 1, -1)):
                q = from_q[1][d]
                await_bytes(v.at[it, q, p, 0 : part.tb], cg_rs.at[it, p, k])
                total = total + applied(p, q)
        for p, part in enumerate(s.parts):
            q = from_q[1][2]
            for k, (lo, hi) in enumerate(part.halves):
                await_bytes(v.at[it, q, p, lo:hi], cg_rs.at[it, p, 3 + k])
            total = total + applied(p, q)

        f_send[it, 0 : s.ft] = as_tiles(total).astype(BF16)
        if s.fz > s.ft:
            f_send[it, s.ft : s.fz] = jnp.zeros((s.fz - s.ft, TILE, LANE), BF16)
        for d in far_first(s.nz):
            piece = f_send.at[it, pl.ds(z_of[d] * s.zp, s.zp)]
            send(piece, f_recv.at[it, d - 1], z_ss.at[it], z_rs.at[it], in_z[d])
        sz_send[it] = to_row(square_sums(it))
        for d in far_first(s.nz):
            send(sz_send.at[it], sz_recv.at[it, d - 1], sz_ss.at[it], sz_rs.at[it], in_z[d])
        await_bytes(f_recv.at[it], z_rs.at[it])
        reduced = f_send[it, pl.ds(z * s.zp, s.zp)].astype(F32)
        for d in range(s.nz - 1):
            reduced = reduced + f_recv[it, d].astype(F32)
        mine = f_all.at[it, pl.ds(z * s.zp, s.zp)]
        mine[...] = reduced.astype(BF16)
        for d in far_first(s.nz):
            send(mine, mine, zg_ss.at[it], zg_rs.at[it], in_z[d])
        await_bytes(sz_recv.at[it], sz_rs.at[it])
        alpha = jnp.sqrt(from_row(sz_send[it] + jnp.sum(sz_recv[it], axis=0), n) + EPSILON)
        alphas[it] = alpha
        inverse[...] = 1.0 / alpha
        ratio = alpha / beta
        await_bytes(f_recv.at[it], zg_rs.at[it])
        for j in range(s.fb):
            lanes = slice(j * LANE, (j + 1) * LANE)
            left[:, lanes] = predicted(it, j) * inverse[...] - left[:, lanes] * ratio
        return carry

    lax.fori_loop(0, 2, iteration, 0)

    sum_start(2, left_sums())
    alpha1, alpha2, beta1, beta2 = alphas[0], alphas[1], betas[0], betas[1]
    rho1 = jnp.sqrt(alpha1 * alpha1 + beta2 * beta2)
    cosine, sine = alpha1 / rho1, beta2 / rho1
    phi1 = cosine * beta1
    phibar = sine * beta1
    theta = sine * alpha2
    rhobar = -cosine * alpha2

    first = place * (s.width // s.rows)
    block = first // LANE
    lane = lax.rem(first, LANE)
    share_width = s.width // s.rows
    cover = -(-share_width // LANE)
    shape = ((cover + 1) * LANE, cover * LANE)
    pick = lax.broadcasted_iota(jnp.int32, shape, 0) == lax.broadcasted_iota(jnp.int32, shape, 1) + lane
    pick = jnp.where(pick, 1.0, 0.0).astype(BF16)
    window = []
    for it in range(2):
        sides = []
        for k in range(cover + 1):
            b = jnp.minimum(block + k, s.width // LANE - 1)
            j = lax.rem(b, s.nb)
            p = j // s.cut
            inside = (j - p * s.cut) * s.groups
            sides.append(v[it, b // s.nb, p, pl.ds(inside, s.groups)].reshape(n, LANE))
        window.append(jnp.dot(jnp.concatenate(sides, axis=1), pick, preferred_element_type=F32))

    sum_middle(2)
    beta3 = sum_end(2)
    rho2 = jnp.sqrt(rhobar * rhobar + beta3 * beta3)
    phi2 = rhobar / rho2 * phibar
    on2 = phi2 / rho2
    weight1 = (phi1 / rho1 - on2 * (theta / rho1)) / alpha1
    weight2 = on2 / alpha2
    result = [weight1 * a + weight2 * b for a, b in zip(lane_blocks(window[0]), lane_blocks(window[1]), strict=True)]
    slip[...] = jnp.concatenate(result, axis=1)[:, 0:share_width]
    for j in range(s.fb):
        lanes = slice(j * LANE, (j + 1) * LANE)
        misfit[:, lanes] = misfit[:, lanes] - weight1 * predicted(0, j) - weight2 * predicted(1, j)

    await_bytes(halo, halo_ss.at[0])

    def settle(it, carry):
        for p, part in enumerate(s.parts):
            four = pc_send.at[it, p, :, 0 : part.tb]
            three = px_send.at[it, p, :, 0 : part.tb]
            pieces = q_recv.at[it, p, :, 0 : part.tp]
            await_bytes(four, c_ss.at[it, p])
            await_bytes(three, x_ss.at[it, p])
            await_bytes(pieces, y_ss.at[it, p])
            await_bytes(pieces, yg_ss.at[it, p])
            await_bytes(three, xg_ss.at[it, p])
            await_bytes(four, cg_ss.at[it, p])
        await_bytes(f_recv.at[it], z_ss.at[it])
        await_bytes(f_recv.at[it], zg_ss.at[it])
        await_bytes(sz_recv.at[it], sz_ss.at[it])
        return carry

    lax.fori_loop(0, 2, settle, 0)
    for i in range(3):
        await_bytes(sa_recv.at[i], sa_ss.at[i])
        await_bytes(sb_recv.at[i], sb_ss.at[i])


def body(dims, nz, data, source, near_tiles, near_rows, near_cols, near_count, far_left, far_right):
    realiz, pixels = data.shape
    rank, width = far_right.shape
    slots, tile_rows, tile_cols = near_tiles.shape
    s = Sizes(dims, nz, realiz, pixels, width, slots, rank, tile_rows, tile_cols)
    vmem = pl.BlockSpec(memory_space=pltpu.VMEM)
    pin = functools.partial(pltpu.with_memory_space_constraint, memory_space=pltpu.HBM)
    return pl.pallas_call(
        functools.partial(kernel, s),
        out_shape=(pltpu.VMEM((realiz, width // s.rows), F32), pltpu.VMEM((realiz, pixels), F32)),
        in_specs=[pl.BlockSpec(memory_space=pl.ANY)] * 8,
        out_specs=(vmem, vmem),
        scratch_shapes=scratch_shapes(s),
        compiler_params=pltpu.CompilerParams(
            collective_id=0, has_side_effects=True, vmem_limit_bytes=48 * 1024 * 1024
        ),
    )(
        pin(data),
        pin(source.reshape(1, pixels)),
        pin(near_rows.reshape(slots)),
        pin(near_cols.reshape(slots)),
        near_count,
        pin(near_tiles),
        pin(far_left),
        pin(far_right),
    )


def solution(mesh, dims=(4, 8, 2)):
    return jax.shard_map(
        functools.partial(body, dims, mesh.shape["cols"]),
        mesh=mesh,
        in_specs=(
            P(None, "rows"),
            P("rows"),
            P("rows", "cols", None),
            P("rows", "cols"),
            P("rows", "cols"),
            P("rows", "cols"),
            P("cols", "rows"),
            P("rows", "cols"),
        ),
        out_specs=(P(None, ("cols", "rows")), P(None, "rows")),
        check_vma=False,
    )
```

```python
import functools

import jax
import jax.numpy as jnp
from jax import lax
from jax.experimental import pallas as pl
from jax.experimental.pallas import tpu as pltpu
from jax.sharding import PartitionSpec as P

EPSILON = 1e-06
LANE = 128
TILE = 16
MESH = pl.DeviceIdType.MESH
F32 = jnp.float32
BF16 = jnp.bfloat16


class Part:
    def __init__(self, first, blocks, s):
        self.lanes = slice(first * LANE, (first + blocks) * LANE)
        self.blocks = blocks
        self.tb = blocks * s.groups
        self.tp = -(-self.tb // s.ny)
        self.tq = self.tp * s.ny


class Sizes:
    def __init__(self, dims, nz, realiz, pixels, width, slots, rank, tile_rows, tile_cols):
        self.nx, self.ny, self.cores = dims
        self.nz = nz
        self.rows = self.nx * self.ny * self.cores
        self.nq = self.nx * self.cores
        self.realiz, self.pixels, self.width = realiz, pixels, width
        self.slots, self.rank, self.tile_rows, self.tile_cols = slots, rank, tile_rows, tile_cols
        self.groups = realiz // TILE
        self.chunk = width // self.nq
        self.nb = self.chunk // LANE
        self.fb = pixels // LANE
        self.ft = self.fb * self.groups
        self.zp = -(-self.ft // nz)
        self.fz = self.zp * nz
        self.cut = (self.nb + 1) // 2
        self.parts = [Part(0, self.cut, self), Part(self.cut, self.nb - self.cut, self)]
        self.tb = max(p.tb for p in self.parts)
        self.tp = max(p.tp for p in self.parts)
        self.tq = max(p.tq for p in self.parts)


def scratch_shapes(s):
    dma = pltpu.SemaphoreType.DMA
    tile = (TILE, LANE)
    return [
        pltpu.VMEM((s.realiz, s.pixels), F32),
        pltpu.VMEM((1, s.pixels), jnp.int32),
        pltpu.VMEM((s.slots + 1, s.tile_rows, s.tile_cols), BF16),
        pltpu.VMEM((s.rank, s.pixels), BF16),
        pltpu.VMEM((s.rank, s.width), BF16),
        pltpu.SMEM((s.slots,), jnp.int32),
        pltpu.SMEM((s.slots,), jnp.int32),
        pltpu.SMEM((1, 1), jnp.int32),
        pltpu.VMEM((8, LANE), jnp.int32),
        pltpu.SMEM((8, LANE), jnp.int32),
        pltpu.VMEM((2, s.realiz, s.pixels), F32),
        pltpu.VMEM((3, s.pixels, s.pixels), BF16),
        pltpu.VMEM((s.nq, s.pixels, s.chunk), BF16),
        pltpu.VMEM((2, 2, s.nx, s.tb, *tile), BF16),
        pltpu.VMEM((2, 2, s.nx, s.tb, *tile), BF16),
        pltpu.VMEM((2, 2, s.nx - 1, s.tb, *tile), BF16),
        pltpu.VMEM((2, 2, s.nx - 1, s.tb, *tile), BF16),
        pltpu.VMEM((2, 2, s.tq, *tile), BF16),
        pltpu.VMEM((2, 2, s.ny - 1, s.tp, *tile), BF16),
        pltpu.VMEM((2, s.nq, 2, s.tq, *tile), BF16),
        pltpu.VMEM((2, s.fz, *tile), BF16),
        pltpu.VMEM((2, s.nz - 1, s.zp, *tile), BF16),
        pltpu.VMEM((2, s.fz, *tile), BF16),
        pltpu.VMEM((s.realiz, s.pixels), F32),
        pltpu.VMEM((2, s.realiz, LANE), F32),
        pltpu.VMEM((2, s.realiz, LANE), F32),
        pltpu.VMEM((s.realiz, LANE), F32),
        pltpu.VMEM((2, s.tp, *tile), F32),
        pltpu.VMEM((2, s.groups, *tile), F32),
        pltpu.VMEM((3, 8, LANE), F32),
        pltpu.VMEM((3, s.nq - 1, 8, LANE), F32),
        pltpu.VMEM((3, 8, LANE), F32),
        pltpu.VMEM((3, s.ny - 1, 8, LANE), F32),
        pltpu.VMEM((2, 8, LANE), F32),
        pltpu.VMEM((2, s.nz - 1, 8, LANE), F32),
        dma((9,)),
        dma((1,)),
        dma((2,)),
        dma((2, 2)),
        dma((2, 2, s.nx)),
        dma((2, 2)),
        dma((2, 2, s.nx - 1)),
        dma((2, 2)),
        dma((2, 2)),
        dma((2, 2)),
        dma((2, 2)),
        dma((2, 2)),
        dma((2, 2, s.nx - 1)),
        dma((2, 2)),
        dma((2, 2, s.nx)),
        dma((2,)),
        dma((2,)),
        dma((2,)),
        dma((2,)),
        dma((3,)),
        dma((3,)),
        dma((3,)),
        dma((3,)),
        dma((2,)),
        dma((2,)),
    ]


def far_first(count):
    return sorted(range(1, count), key=lambda d: (-min(d, count - d), d))


def near_first(count):
    return sorted(range(1, count), key=lambda d: (min(d, count - d), d))


def await_bytes(ref, sem):
    pltpu.make_async_copy(ref, ref, sem).wait()


def to_row(column):
    rows = column.shape[0]
    wide = jnp.broadcast_to(column, (rows, LANE))
    wide = jnp.concatenate([wide, jnp.zeros((LANE - rows, LANE), F32)], axis=0)
    return wide.T[0:8]


def from_row(row, rows):
    return jnp.broadcast_to(row[0:1], (LANE, LANE)).T[0:rows]


def row_sums(blocks):
    total = blocks[0] * blocks[0]
    for block in blocks[1:]:
        total = total + block * block
    return jnp.sum(total, axis=1, keepdims=True)


def lane_blocks(value):
    return [value[:, j * LANE : (j + 1) * LANE] for j in range(value.shape[1] // LANE)]


def as_tiles(value):
    groups = value.shape[0] // TILE
    return jnp.concatenate([b.reshape(groups, TILE, LANE) for b in lane_blocks(value)], axis=0)


def from_tiles(tiles, groups):
    count = tiles.shape[0] // groups
    return jnp.concatenate(
        [tiles[j * groups : (j + 1) * groups].reshape(groups * TILE, LANE) for j in range(count)], axis=1
    )


def three_parts(value):
    high = value.astype(BF16)
    rest = value - high.astype(F32)
    middle = rest.astype(BF16)
    low = (rest - middle.astype(F32)).astype(BF16)
    return jnp.concatenate([high, middle, low], axis=0)


def kernel(
    s, data_hbm, source_hbm, rows_hbm, cols_hbm, count_hbm, tiles_hbm, left_hbm, right_hbm, slip, misfit,
    data, source, tiles, far_left, far_right, near_rows, near_cols, near_count, table, table_s, halo, onehot, g,
    pc_send, pc_recv, px_send, px_recv, q_send, q_recv, v, f_send, f_recv, f_all, left, alphas, betas, inverse,
    previous, coef, sa_send, sa_recv, sb_send, sb_recv, sz_send, sz_recv, in_sem, halo_ss, halo_rs, c_ss, c_rs,
    x_ss, x_rs, y_ss, y_rs, yg_ss, yg_rs, xg_ss, xg_rs, cg_ss, cg_rs, z_ss, z_rs, zg_ss, zg_rs, sa_ss, sa_rs,
    sb_ss, sb_rs, sz_ss, sz_rs,
):
    place = lax.axis_index("rows")
    z = lax.axis_index("cols")
    core = lax.rem(place, 2)
    chip = place // 2
    y = lax.rem(chip, s.ny)
    x = chip // s.ny
    other = 1 - core
    own_q = core * s.nx + x
    n = s.realiz

    def at(xx, yy, cc):
        return ((xx * s.ny + yy) * 2 + cc, z)

    def cross(d):
        q = lax.rem(own_q + d, s.nq)
        return at(lax.rem(q, s.nx), y, q // s.nx)

    def beside(d):
        return lax.rem(x + d + s.nx, s.nx)

    mate = at(x, y, other)
    crosses = [None] + [cross(d) for d in range(1, s.nq)]
    in_x = [None] + [at(beside(d), y, core) for d in range(1, s.nx)]
    y_of = [lax.rem(y + d, s.ny) for d in range(s.ny)]
    in_y = [None] + [at(x, y_of[d], core) for d in range(1, s.ny)]
    z_of = [lax.rem(z + d, s.nz) for d in range(s.nz)]
    in_z = [None] + [(place, z_of[d]) for d in range(1, s.nz)]
    to_q = [[cc * s.nx + beside(d) for d in range(s.nx)] for cc in (core, other)]
    from_q = [[cc * s.nx + beside(-d) for d in range(s.nx)] for cc in (core, other)]

    def send(src, dst, send_sem, recv_sem, device):
        pltpu.make_async_remote_copy(
            src_ref=src, dst_ref=dst, send_sem=send_sem, recv_sem=recv_sem, device_id=device, device_id_type=MESH
        ).start()

    step_out = lax.rem(place + s.rows + 2 * core - 1, s.rows)
    partners = crosses[1:] + in_y[1:] + in_z[1:]
    partners += [(step_out, z)]
    barrier = pltpu.get_barrier_semaphore()
    for device in partners:
        pl.semaphore_signal(barrier, inc=1, device_id=device, device_id_type=MESH)

    pairs = [
        (rows_hbm, near_rows),
        (cols_hbm, near_cols),
        (count_hbm, near_count),
        (source_hbm, source),
        (data_hbm, data),
        (left_hbm, far_left),
        (right_hbm, far_right),
        (tiles_hbm, tiles.at[0 : s.slots]),
    ]
    loads = [pltpu.make_async_copy(src, dst, in_sem.at[k]) for k, (src, dst) in enumerate(pairs)]
    for load in loads:
        load.start()

    pl.semaphore_wait(barrier, len(partners))

    after = lax.rem(place + 1, s.rows)
    before = lax.rem(place + s.rows - 1, s.rows)
    send(data_hbm, halo.at[0], halo_ss.at[0], halo_rs.at[0], (after, z))
    send(data_hbm, halo.at[1], halo_ss.at[0], halo_rs.at[1], (before, z))

    tiles[s.slots] = jnp.zeros((s.tile_rows, s.tile_cols), BF16)
    for load in loads[:3]:
        load.wait()
    per_row = s.width // s.tile_cols
    spot = lax.broadcasted_iota(jnp.int32, (8, LANE), 1)
    slot_of = jnp.full((8, LANE), s.slots, jnp.int32)
    for k in range(s.slots):
        where = jnp.where(k < near_count[0, 0], near_rows[k] * per_row + near_cols[k], -1)
        slot_of = jnp.where(spot == where, k, slot_of)
    table[...] = slot_of
    to_scalars = pltpu.make_async_copy(table, table_s, in_sem.at[8])
    to_scalars.start()

    loads[3].wait()
    total = s.rows * s.pixels
    offset = source[...] + s.pixels - place * s.pixels
    offset = jnp.where(offset < 0, offset + total, offset)
    offset = jnp.where(offset >= total, offset - total, offset)
    index = lax.broadcasted_iota(jnp.int32, (s.pixels, s.pixels), 0)
    for k in range(3):
        onehot[k] = jnp.where(index == offset - k * s.pixels, 1.0, 0.0).astype(BF16)

    for load in loads[4:]:
        load.wait()
    to_scalars.wait()
    half = per_row // 2
    half_blocks = half * s.tile_cols // LANE
    bands = s.pixels // s.tile_rows

    def build(i, carry):
        side, a = i // bands, lax.rem(i, bands)
        pixel = pl.ds(pl.multiple_of(a * s.tile_rows, s.tile_rows), s.tile_rows)
        lefts = far_left[:, pixel]
        for b in range(half):
            column = pl.ds(pl.multiple_of((side * half + b) * s.tile_cols, s.tile_cols), s.tile_cols)
            block = lax.dot_general(lefts, far_right[:, column], (((0,), (0,)), ((), ())), preferred_element_type=F32)
            near = tiles[table_s[0, a * per_row + side * half + b]]
            block = (block + near.astype(F32)).astype(BF16)
            for k in range(s.tile_cols // LANE):
                j = b * (s.tile_cols // LANE) + k
                q = side * (half_blocks // s.nb) + j // s.nb
                lane = (j % s.nb) * LANE
                g[q, pixel, lane : lane + LANE] = block[:, k * LANE : (k + 1) * LANE]
        return carry

    lax.fori_loop(0, 2 * bands, build, 0)

    seen = jnp.dot(three_parts(data[...]), onehot[1], preferred_element_type=F32)
    for k in range(2):
        await_bytes(halo.at[k], halo_rs.at[k])
        seen = seen + jnp.dot(three_parts(halo[k]), onehot[2 * k], preferred_element_type=F32)
    observed = (seen[0:n] + seen[n : 2 * n]) + seen[2 * n : 3 * n]
    misfit[...] = observed
    left[...] = observed
    previous[...] = jnp.zeros_like(previous)
    inverse[...] = jnp.zeros_like(inverse)

    def sum_start(i, column):
        sa_send[i] = to_row(column)
        for d in range(1, s.nq):
            send(sa_send.at[i], sa_recv.at[i, d - 1], sa_ss.at[i], sa_rs.at[i], crosses[d])

    def sum_middle(i):
        await_bytes(sa_recv.at[i], sa_rs.at[i])
        sb_send[i] = sa_send[i] + jnp.sum(sa_recv[i], axis=0)
        for d in range(1, s.ny):
            send(sb_send.at[i], sb_recv.at[i, d - 1], sb_ss.at[i], sb_rs.at[i], in_y[d])

    def sum_end(i):
        await_bytes(sb_recv.at[i], sb_rs.at[i])
        return jnp.sqrt(from_row(sb_send[i] + jnp.sum(sb_recv[i], axis=0), n) + EPSILON)

    def square_sums(it):
        def squares(q, running):
            for p, part in enumerate(s.parts):
                for j in range(part.blocks):
                    block = v[it, q, p, j * s.groups : (j + 1) * s.groups].astype(F32).reshape(n, LANE)
                    running = running + block * block
            return running

        running = lax.fori_loop(0, s.nq, squares, jnp.zeros((n, LANE), F32))
        return jnp.sum(running, axis=1, keepdims=True)

    def predicted(it, j):
        return f_all[it, j * s.groups : (j + 1) * s.groups].astype(F32).reshape(n, LANE)

    def left_sums():
        return row_sums(lane_blocks(left[...]))

    def iteration(it, carry):
        pixel_b = left[...].astype(BF16)

        def product(p, q):
            return as_tiles(jnp.dot(pixel_b, g[q, :, s.parts[p].lanes], preferred_element_type=F32))

        def to_mate(p, d):
            tb = s.parts[p].tb
            mine = pc_send.at[it, p, d, 0:tb]
            mine[...] = product(p, to_q[1][d]).astype(BF16)
            send(mine, pc_recv.at[it, p, d, 0:tb], c_ss.at[it, p], c_rs.at[it, p, d], mate)

        def pair_sum(p, d):
            own = product(p, to_q[0][d])
            came = pc_recv.at[it, p, d, 0 : s.parts[p].tb]
            await_bytes(came, c_rs.at[it, p, d])
            return own + came[...].astype(F32)

        def scatter_x(p, d):
            mine = px_send.at[it, p, d - 1, 0 : s.parts[p].tb]
            mine[...] = pair_sum(p, d).astype(BF16)
            send(mine, px_recv.at[it, p, d - 1, 0 : s.parts[p].tb], x_ss.at[it, p], x_rs.at[it, p, d - 1], in_x[d])

        def scatter_y(p):
            tb, tp, tq = s.parts[p].tb, s.parts[p].tp, s.parts[p].tq
            own = pair_sum(p, 0)
            for d in near_first(s.nx):
                came = px_recv.at[it, p, d - 1, 0:tb]
                await_bytes(came, x_rs.at[it, p, d - 1])
                own = own + came[...].astype(F32)
            q_send[it, p, 0:tb] = own.astype(BF16)
            if tq > tb:
                q_send[it, p, tb:tq] = jnp.zeros((tq - tb, TILE, LANE), BF16)
            for d in far_first(s.ny):
                piece = q_send.at[it, p, pl.ds(y_of[d] * tp, tp)]
                send(piece, q_recv.at[it, p, d - 1, 0:tp], y_ss.at[it, p], y_rs.at[it, p], in_y[d])

        def spread_y(p):
            tp = s.parts[p].tp
            await_bytes(q_recv.at[it, p, :, 0:tp], y_rs.at[it, p])
            share = q_send[it, p, pl.ds(y * tp, tp)].astype(F32)
            for d in range(s.ny - 1):
                share = share + q_recv[it, p, d, 0:tp].astype(F32)
            mine = v.at[it, own_q, p, pl.ds(y * tp, tp)]
            for i in range(tp):
                group = lax.rem(y * tp + i, s.groups)
                raw = share[i] * coef[0, group] - previous[p, i] * coef[1, group]
                previous[p, i] = raw
                v[it, own_q, p, y * tp + i] = raw.astype(BF16)
            for d in far_first(s.ny):
                send(mine, mine, yg_ss.at[it, p], yg_rs.at[it, p], in_y[d])

        def applied(p, q):
            return lax.dot_general(
                from_tiles(v[it, q, p, 0 : s.parts[p].tb], s.groups),
                g[q, :, s.parts[p].lanes],
                (((1,), (1,)), ((), ())),
                preferred_element_type=F32,
            )

        order = far_first(s.nx)
        for d in order:
            to_mate(0, d)
        sum_start(it, left_sums())
        for d in order:
            to_mate(1, d)
            scatter_x(0, d)
        to_mate(0, 0)
        to_mate(1, 0)
        for d in order:
            scatter_x(1, d)
        scatter_y(0)
        sum_middle(it)
        scatter_y(1)
        beta = sum_end(it)
        betas[it] = beta
        coef[0] = (1.0 / beta).reshape(s.groups, TILE, LANE)
        coef[1] = (beta * inverse[...]).reshape(s.groups, TILE, LANE)
        for p in range(2):
            spread_y(p)

        total = jnp.zeros((n, s.pixels), F32)
        for p, part in enumerate(s.parts):
            await_bytes(q_recv.at[it, p, :, 0 : part.tp], yg_rs.at[it, p])
            ready = v.at[it, own_q, p, 0 : part.tb]
            for d in far_first(s.nx):
                send(ready, ready, xg_ss.at[it, p], xg_rs.at[it, p, d - 1], in_x[d])
            send(ready, ready, cg_ss.at[it, p], cg_rs.at[it, p, 0], mate)
            total = total + applied(p, own_q)
        for p, part in enumerate(s.parts):
            for d in near_first(s.nx):
                q = from_q[0][d]
                came = v.at[it, q, p, 0 : part.tb]
                await_bytes(came, xg_rs.at[it, p, d - 1])
                send(came, came, cg_ss.at[it, p], cg_rs.at[it, p, d], mate)
                total = total + applied(p, q)
        for p, part in enumerate(s.parts):
            for d in [0] + near_first(s.nx):
                q = from_q[1][d]
                await_bytes(v.at[it, q, p, 0 : part.tb], cg_rs.at[it, p, d])
                total = total + applied(p, q)

        f_send[it, 0 : s.ft] = as_tiles(total).astype(BF16)
        if s.fz > s.ft:
            f_send[it, s.ft : s.fz] = jnp.zeros((s.fz - s.ft, TILE, LANE), BF16)
        for d in far_first(s.nz):
            piece = f_send.at[it, pl.ds(z_of[d] * s.zp, s.zp)]
            send(piece, f_recv.at[it, d - 1], z_ss.at[it], z_rs.at[it], in_z[d])
        sz_send[it] = to_row(square_sums(it))
        for d in far_first(s.nz):
            send(sz_send.at[it], sz_recv.at[it, d - 1], sz_ss.at[it], sz_rs.at[it], in_z[d])
        await_bytes(f_recv.at[it], z_rs.at[it])
        reduced = f_send[it, pl.ds(z * s.zp, s.zp)].astype(F32)
        for d in range(s.nz - 1):
            reduced = reduced + f_recv[it, d].astype(F32)
        mine = f_all.at[it, pl.ds(z * s.zp, s.zp)]
        mine[...] = reduced.astype(BF16)
        for d in far_first(s.nz):
            send(mine, mine, zg_ss.at[it], zg_rs.at[it], in_z[d])
        await_bytes(sz_recv.at[it], sz_rs.at[it])
        alpha = jnp.sqrt(from_row(sz_send[it] + jnp.sum(sz_recv[it], axis=0), n) + EPSILON)
        alphas[it] = alpha
        inverse[...] = 1.0 / alpha
        ratio = alpha / beta
        await_bytes(f_recv.at[it], zg_rs.at[it])
        for j in range(s.fb):
            lanes = slice(j * LANE, (j + 1) * LANE)
            left[:, lanes] = predicted(it, j) * inverse[...] - left[:, lanes] * ratio
        return carry

    lax.fori_loop(0, 2, iteration, 0)

    sum_start(2, left_sums())
    alpha1, alpha2, beta1, beta2 = alphas[0], alphas[1], betas[0], betas[1]
    rho1 = jnp.sqrt(alpha1 * alpha1 + beta2 * beta2)
    cosine, sine = alpha1 / rho1, beta2 / rho1
    phi1 = cosine * beta1
    phibar = sine * beta1
    theta = sine * alpha2
    rhobar = -cosine * alpha2

    first = place * (s.width // s.rows)
    block = first // LANE
    lane = lax.rem(first, LANE)
    share_width = s.width // s.rows
    cover = -(-share_width // LANE)
    shape = ((cover + 1) * LANE, cover * LANE)
    pick = lax.broadcasted_iota(jnp.int32, shape, 0) == lax.broadcasted_iota(jnp.int32, shape, 1) + lane
    pick = jnp.where(pick, 1.0, 0.0).astype(BF16)
    window = []
    for it in range(2):
        sides = []
        for k in range(cover + 1):
            b = jnp.minimum(block + k, s.width // LANE - 1)
            j = lax.rem(b, s.nb)
            p = j // s.cut
            inside = (j - p * s.cut) * s.groups
            sides.append(v[it, b // s.nb, p, pl.ds(inside, s.groups)].reshape(n, LANE))
        window.append(jnp.dot(jnp.concatenate(sides, axis=1), pick, preferred_element_type=F32))

    sum_middle(2)
    beta3 = sum_end(2)
    rho2 = jnp.sqrt(rhobar * rhobar + beta3 * beta3)
    phi2 = rhobar / rho2 * phibar
    on2 = phi2 / rho2
    weight1 = (phi1 / rho1 - on2 * (theta / rho1)) / alpha1
    weight2 = on2 / alpha2
    result = [weight1 * a + weight2 * b for a, b in zip(lane_blocks(window[0]), lane_blocks(window[1]), strict=True)]
    slip[...] = jnp.concatenate(result, axis=1)[:, 0:share_width]
    for j in range(s.fb):
        lanes = slice(j * LANE, (j + 1) * LANE)
        misfit[:, lanes] = misfit[:, lanes] - weight1 * predicted(0, j) - weight2 * predicted(1, j)

    await_bytes(halo, halo_ss.at[0])

    def settle(it, carry):
        for p, part in enumerate(s.parts):
            four = pc_send.at[it, p, :, 0 : part.tb]
            three = px_send.at[it, p, :, 0 : part.tb]
            pieces = q_recv.at[it, p, :, 0 : part.tp]
            await_bytes(four, c_ss.at[it, p])
            await_bytes(three, x_ss.at[it, p])
            await_bytes(pieces, y_ss.at[it, p])
            await_bytes(pieces, yg_ss.at[it, p])
            await_bytes(three, xg_ss.at[it, p])
            await_bytes(four, cg_ss.at[it, p])
        await_bytes(f_recv.at[it], z_ss.at[it])
        await_bytes(f_recv.at[it], zg_ss.at[it])
        await_bytes(sz_recv.at[it], sz_ss.at[it])
        return carry

    lax.fori_loop(0, 2, settle, 0)
    for i in range(3):
        await_bytes(sa_recv.at[i], sa_ss.at[i])
        await_bytes(sb_recv.at[i], sb_ss.at[i])


def body(dims, nz, data, source, near_tiles, near_rows, near_cols, near_count, far_left, far_right):
    realiz, pixels = data.shape
    rank, width = far_right.shape
    slots, tile_rows, tile_cols = near_tiles.shape
    s = Sizes(dims, nz, realiz, pixels, width, slots, rank, tile_rows, tile_cols)
    vmem = pl.BlockSpec(memory_space=pltpu.VMEM)
    pin = functools.partial(pltpu.with_memory_space_constraint, memory_space=pltpu.HBM)
    return pl.pallas_call(
        functools.partial(kernel, s),
        out_shape=(pltpu.VMEM((realiz, width // s.rows), F32), pltpu.VMEM((realiz, pixels), F32)),
        in_specs=[pl.BlockSpec(memory_space=pl.ANY)] * 8,
        out_specs=(vmem, vmem),
        scratch_shapes=scratch_shapes(s),
        compiler_params=pltpu.CompilerParams(
            collective_id=0, has_side_effects=True, vmem_limit_bytes=48 * 1024 * 1024
        ),
    )(
        pin(data),
        pin(source.reshape(1, pixels)),
        pin(near_rows.reshape(slots)),
        pin(near_cols.reshape(slots)),
        near_count,
        pin(near_tiles),
        pin(far_left),
        pin(far_right),
    )


def solution(mesh, dims=(4, 8, 2)):
    return jax.shard_map(
        functools.partial(body, dims, mesh.shape["cols"]),
        mesh=mesh,
        in_specs=(
            P(None, "rows"),
            P("rows"),
            P("rows", "cols", None),
            P("rows", "cols"),
            P("rows", "cols"),
            P("rows", "cols"),
            P("cols", "rows"),
            P("rows", "cols"),
        ),
        out_specs=(P(None, ("cols", "rows")), P(None, "rows")),
        check_vma=False,
    )
```

```python
import functools

import jax
import jax.numpy as jnp
from jax import lax
from jax.experimental import pallas as pl
from jax.experimental.pallas import tpu as pltpu
from jax.sharding import PartitionSpec as P

EPSILON = 1e-06
LANE = 128
TILE = 16
MESH = pl.DeviceIdType.MESH
F32 = jnp.float32
BF16 = jnp.bfloat16


class Part:
    def __init__(self, first, blocks, s):
        self.lanes = slice(first * LANE, (first + blocks) * LANE)
        self.blocks = blocks
        self.tb = blocks * s.groups
        self.tp = -(-self.tb // s.ny)
        self.tq = self.tp * s.ny


class Sizes:
    def __init__(self, dims, nz, realiz, pixels, width, slots, rank, tile_rows, tile_cols):
        self.nx, self.ny, self.cores = dims
        self.nz = nz
        self.rows = self.nx * self.ny * self.cores
        self.nq = self.nx * self.cores
        self.realiz, self.pixels, self.width = realiz, pixels, width
        self.slots, self.rank, self.tile_rows, self.tile_cols = slots, rank, tile_rows, tile_cols
        self.groups = realiz // TILE
        self.chunk = width // self.nq
        self.nb = self.chunk // LANE
        self.fb = pixels // LANE
        self.ft = self.fb * self.groups
        self.zp = -(-self.ft // nz)
        self.fz = self.zp * nz
        self.cut = self.nb
        self.parts = [Part(0, self.nb, self)]
        self.tb = max(p.tb for p in self.parts)
        self.tp = max(p.tp for p in self.parts)
        self.tq = max(p.tq for p in self.parts)


def scratch_shapes(s):
    dma = pltpu.SemaphoreType.DMA
    tile = (TILE, LANE)
    return [
        pltpu.VMEM((s.realiz, s.pixels), F32),
        pltpu.VMEM((1, s.pixels), jnp.int32),
        pltpu.VMEM((s.slots + 1, s.tile_rows, s.tile_cols), BF16),
        pltpu.VMEM((s.rank, s.pixels), BF16),
        pltpu.VMEM((s.rank, s.width), BF16),
        pltpu.SMEM((s.slots,), jnp.int32),
        pltpu.SMEM((s.slots,), jnp.int32),
        pltpu.SMEM((1, 1), jnp.int32),
        pltpu.VMEM((8, LANE), jnp.int32),
        pltpu.SMEM((8, LANE), jnp.int32),
        pltpu.VMEM((2, s.realiz, s.pixels), F32),
        pltpu.VMEM((3, s.pixels, s.pixels), BF16),
        pltpu.VMEM((s.nq, s.pixels, s.chunk), BF16),
        pltpu.VMEM((2, len(s.parts), s.nx, s.tb, *tile), BF16),
        pltpu.VMEM((2, len(s.parts), s.nx, s.tb, *tile), BF16),
        pltpu.VMEM((2, len(s.parts), s.nx - 1, s.tb, *tile), BF16),
        pltpu.VMEM((2, len(s.parts), s.nx - 1, s.tb, *tile), BF16),
        pltpu.VMEM((2, len(s.parts), s.tq, *tile), BF16),
        pltpu.VMEM((2, len(s.parts), s.ny - 1, s.tp, *tile), BF16),
        pltpu.VMEM((2, s.nq, len(s.parts), s.tq, *tile), BF16),
        pltpu.VMEM((2, s.fz, *tile), BF16),
        pltpu.VMEM((2, s.nz - 1, s.zp, *tile), BF16),
        pltpu.VMEM((2, s.fz, *tile), BF16),
        pltpu.VMEM((s.realiz, s.pixels), F32),
        pltpu.VMEM((2, s.realiz, LANE), F32),
        pltpu.VMEM((2, s.realiz, LANE), F32),
        pltpu.VMEM((s.realiz, LANE), F32),
        pltpu.VMEM((len(s.parts), s.tp, *tile), F32),
        pltpu.VMEM((2, s.groups, *tile), F32),
        pltpu.VMEM((3, 8, LANE), F32),
        pltpu.VMEM((3, s.nq - 1, 8, LANE), F32),
        pltpu.VMEM((3, 8, LANE), F32),
        pltpu.VMEM((3, s.ny - 1, 8, LANE), F32),
        pltpu.VMEM((2, 8, LANE), F32),
        pltpu.VMEM((2, s.nz - 1, 8, LANE), F32),
        dma((9,)),
        dma((1,)),
        dma((2,)),
        dma((2, 2)),
        dma((2, len(s.parts), s.nx)),
        dma((2, 2)),
        dma((2, len(s.parts), s.nx - 1)),
        dma((2, 2)),
        dma((2, 2)),
        dma((2, 2)),
        dma((2, 2)),
        dma((2, 2)),
        dma((2, len(s.parts), s.nx - 1)),
        dma((2, 2)),
        dma((2, len(s.parts), s.nx)),
        dma((2,)),
        dma((2,)),
        dma((2,)),
        dma((2,)),
        dma((3,)),
        dma((3,)),
        dma((3,)),
        dma((3,)),
        dma((2,)),
        dma((2,)),
    ]


def far_first(count):
    return sorted(range(1, count), key=lambda d: (-min(d, count - d), d))


def near_first(count):
    return sorted(range(1, count), key=lambda d: (min(d, count - d), d))


def await_bytes(ref, sem):
    pltpu.make_async_copy(ref, ref, sem).wait()


def to_row(column):
    rows = column.shape[0]
    wide = jnp.broadcast_to(column, (rows, LANE))
    wide = jnp.concatenate([wide, jnp.zeros((LANE - rows, LANE), F32)], axis=0)
    return wide.T[0:8]


def from_row(row, rows):
    return jnp.broadcast_to(row[0:1], (LANE, LANE)).T[0:rows]


def row_sums(blocks):
    total = blocks[0] * blocks[0]
    for block in blocks[1:]:
        total = total + block * block
    return jnp.sum(total, axis=1, keepdims=True)


def lane_blocks(value):
    return [value[:, j * LANE : (j + 1) * LANE] for j in range(value.shape[1] // LANE)]


def as_tiles(value):
    groups = value.shape[0] // TILE
    return jnp.concatenate([b.reshape(groups, TILE, LANE) for b in lane_blocks(value)], axis=0)


def from_tiles(tiles, groups):
    count = tiles.shape[0] // groups
    return jnp.concatenate(
        [tiles[j * groups : (j + 1) * groups].reshape(groups * TILE, LANE) for j in range(count)], axis=1
    )


def three_parts(value):
    high = value.astype(BF16)
    rest = value - high.astype(F32)
    middle = rest.astype(BF16)
    low = (rest - middle.astype(F32)).astype(BF16)
    return jnp.concatenate([high, middle, low], axis=0)


def kernel(
    s, data_hbm, source_hbm, rows_hbm, cols_hbm, count_hbm, tiles_hbm, left_hbm, right_hbm, slip, misfit,
    data, source, tiles, far_left, far_right, near_rows, near_cols, near_count, table, table_s, halo, onehot, g,
    pc_send, pc_recv, px_send, px_recv, q_send, q_recv, v, f_send, f_recv, f_all, left, alphas, betas, inverse,
    previous, coef, sa_send, sa_recv, sb_send, sb_recv, sz_send, sz_recv, in_sem, halo_ss, halo_rs, c_ss, c_rs,
    x_ss, x_rs, y_ss, y_rs, yg_ss, yg_rs, xg_ss, xg_rs, cg_ss, cg_rs, z_ss, z_rs, zg_ss, zg_rs, sa_ss, sa_rs,
    sb_ss, sb_rs, sz_ss, sz_rs,
):
    place = lax.axis_index("rows")
    z = lax.axis_index("cols")
    core = lax.rem(place, 2)
    chip = place // 2
    y = lax.rem(chip, s.ny)
    x = chip // s.ny
    other = 1 - core
    own_q = core * s.nx + x
    n = s.realiz

    def at(xx, yy, cc):
        return ((xx * s.ny + yy) * 2 + cc, z)

    def cross(d):
        q = lax.rem(own_q + d, s.nq)
        return at(lax.rem(q, s.nx), y, q // s.nx)

    def beside(d):
        return lax.rem(x + d + s.nx, s.nx)

    mate = at(x, y, other)
    crosses = [None] + [cross(d) for d in range(1, s.nq)]
    in_x = [None] + [at(beside(d), y, core) for d in range(1, s.nx)]
    y_of = [lax.rem(y + d, s.ny) for d in range(s.ny)]
    in_y = [None] + [at(x, y_of[d], core) for d in range(1, s.ny)]
    z_of = [lax.rem(z + d, s.nz) for d in range(s.nz)]
    in_z = [None] + [(place, z_of[d]) for d in range(1, s.nz)]
    to_q = [[cc * s.nx + beside(d) for d in range(s.nx)] for cc in (core, other)]
    from_q = [[cc * s.nx + beside(-d) for d in range(s.nx)] for cc in (core, other)]

    def send(src, dst, send_sem, recv_sem, device):
        pltpu.make_async_remote_copy(
            src_ref=src, dst_ref=dst, send_sem=send_sem, recv_sem=recv_sem, device_id=device, device_id_type=MESH
        ).start()

    step_out = lax.rem(place + s.rows + 2 * core - 1, s.rows)
    partners = crosses[1:] + in_y[1:] + in_z[1:]
    partners += [(step_out, z)]
    barrier = pltpu.get_barrier_semaphore()
    for device in partners:
        pl.semaphore_signal(barrier, inc=1, device_id=device, device_id_type=MESH)

    pairs = [
        (rows_hbm, near_rows),
        (cols_hbm, near_cols),
        (count_hbm, near_count),
        (source_hbm, source),
        (data_hbm, data),
        (left_hbm, far_left),
        (right_hbm, far_right),
        (tiles_hbm, tiles.at[0 : s.slots]),
    ]
    loads = [pltpu.make_async_copy(src, dst, in_sem.at[k]) for k, (src, dst) in enumerate(pairs)]
    for load in loads:
        load.start()

    pl.semaphore_wait(barrier, len(partners))

    after = lax.rem(place + 1, s.rows)
    before = lax.rem(place + s.rows - 1, s.rows)
    send(data_hbm, halo.at[0], halo_ss.at[0], halo_rs.at[0], (after, z))
    send(data_hbm, halo.at[1], halo_ss.at[0], halo_rs.at[1], (before, z))

    tiles[s.slots] = jnp.zeros((s.tile_rows, s.tile_cols), BF16)
    for load in loads[:3]:
        load.wait()
    per_row = s.width // s.tile_cols
    spot = lax.broadcasted_iota(jnp.int32, (8, LANE), 1)
    slot_of = jnp.full((8, LANE), s.slots, jnp.int32)
    for k in range(s.slots):
        where = jnp.where(k < near_count[0, 0], near_rows[k] * per_row + near_cols[k], -1)
        slot_of = jnp.where(spot == where, k, slot_of)
    table[...] = slot_of
    to_scalars = pltpu.make_async_copy(table, table_s, in_sem.at[8])
    to_scalars.start()

    loads[3].wait()
    total = s.rows * s.pixels
    offset = source[...] + s.pixels - place * s.pixels
    offset = jnp.where(offset < 0, offset + total, offset)
    offset = jnp.where(offset >= total, offset - total, offset)
    index = lax.broadcasted_iota(jnp.int32, (s.pixels, s.pixels), 0)
    for k in range(3):
        onehot[k] = jnp.where(index == offset - k * s.pixels, 1.0, 0.0).astype(BF16)

    for load in loads[4:]:
        load.wait()
    to_scalars.wait()
    half = per_row // 2
    half_blocks = half * s.tile_cols // LANE
    bands = s.pixels // s.tile_rows

    def build(i, carry):
        side, a = i // bands, lax.rem(i, bands)
        pixel = pl.ds(pl.multiple_of(a * s.tile_rows, s.tile_rows), s.tile_rows)
        lefts = far_left[:, pixel]
        for b in range(half):
            column = pl.ds(pl.multiple_of((side * half + b) * s.tile_cols, s.tile_cols), s.tile_cols)
            block = lax.dot_general(lefts, far_right[:, column], (((0,), (0,)), ((), ())), preferred_element_type=F32)
            near = tiles[table_s[0, a * per_row + side * half + b]]
            block = (block + near.astype(F32)).astype(BF16)
            for k in range(s.tile_cols // LANE):
                j = b * (s.tile_cols // LANE) + k
                q = side * (half_blocks // s.nb) + j // s.nb
                lane = (j % s.nb) * LANE
                g[q, pixel, lane : lane + LANE] = block[:, k * LANE : (k + 1) * LANE]
        return carry

    lax.fori_loop(0, 2 * bands, build, 0)

    seen = jnp.dot(three_parts(data[...]), onehot[1], preferred_element_type=F32)
    for k in range(2):
        await_bytes(halo.at[k], halo_rs.at[k])
        seen = seen + jnp.dot(three_parts(halo[k]), onehot[2 * k], preferred_element_type=F32)
    observed = (seen[0:n] + seen[n : 2 * n]) + seen[2 * n : 3 * n]
    misfit[...] = observed
    left[...] = observed
    previous[...] = jnp.zeros_like(previous)
    inverse[...] = jnp.zeros_like(inverse)

    def sum_start(i, column):
        sa_send[i] = to_row(column)
        for d in range(1, s.nq):
            send(sa_send.at[i], sa_recv.at[i, d - 1], sa_ss.at[i], sa_rs.at[i], crosses[d])

    def sum_middle(i):
        await_bytes(sa_recv.at[i], sa_rs.at[i])
        sb_send[i] = sa_send[i] + jnp.sum(sa_recv[i], axis=0)
        for d in range(1, s.ny):
            send(sb_send.at[i], sb_recv.at[i, d - 1], sb_ss.at[i], sb_rs.at[i], in_y[d])

    def sum_end(i):
        await_bytes(sb_recv.at[i], sb_rs.at[i])
        return jnp.sqrt(from_row(sb_send[i] + jnp.sum(sb_recv[i], axis=0), n) + EPSILON)

    def square_sums(it):
        def squares(q, running):
            for p, part in enumerate(s.parts):
                for j in range(part.blocks):
                    block = v[it, q, p, j * s.groups : (j + 1) * s.groups].astype(F32).reshape(n, LANE)
                    running = running + block * block
            return running

        running = lax.fori_loop(0, s.nq, squares, jnp.zeros((n, LANE), F32))
        return jnp.sum(running, axis=1, keepdims=True)

    def predicted(it, j):
        return f_all[it, j * s.groups : (j + 1) * s.groups].astype(F32).reshape(n, LANE)

    def left_sums():
        return row_sums(lane_blocks(left[...]))

    def iteration(it, carry):
        pixel_b = left[...].astype(BF16)

        def product(p, q):
            return as_tiles(jnp.dot(pixel_b, g[q, :, s.parts[p].lanes], preferred_element_type=F32))

        def to_mate(p, d):
            tb = s.parts[p].tb
            mine = pc_send.at[it, p, d, 0:tb]
            mine[...] = product(p, to_q[1][d]).astype(BF16)
            send(mine, pc_recv.at[it, p, d, 0:tb], c_ss.at[it, p], c_rs.at[it, p, d], mate)

        def pair_sum(p, d):
            own = product(p, to_q[0][d])
            came = pc_recv.at[it, p, d, 0 : s.parts[p].tb]
            await_bytes(came, c_rs.at[it, p, d])
            return own + came[...].astype(F32)

        def scatter_x(p, d):
            mine = px_send.at[it, p, d - 1, 0 : s.parts[p].tb]
            mine[...] = pair_sum(p, d).astype(BF16)
            send(mine, px_recv.at[it, p, d - 1, 0 : s.parts[p].tb], x_ss.at[it, p], x_rs.at[it, p, d - 1], in_x[d])

        def scatter_y(p):
            tb, tp, tq = s.parts[p].tb, s.parts[p].tp, s.parts[p].tq
            own = pair_sum(p, 0)
            for d in near_first(s.nx):
                came = px_recv.at[it, p, d - 1, 0:tb]
                await_bytes(came, x_rs.at[it, p, d - 1])
                own = own + came[...].astype(F32)
            q_send[it, p, 0:tb] = own.astype(BF16)
            if tq > tb:
                q_send[it, p, tb:tq] = jnp.zeros((tq - tb, TILE, LANE), BF16)
            for d in far_first(s.ny):
                piece = q_send.at[it, p, pl.ds(y_of[d] * tp, tp)]
                send(piece, q_recv.at[it, p, d - 1, 0:tp], y_ss.at[it, p], y_rs.at[it, p], in_y[d])

        def spread_y(p):
            tp = s.parts[p].tp
            await_bytes(q_recv.at[it, p, :, 0:tp], y_rs.at[it, p])
            share = q_send[it, p, pl.ds(y * tp, tp)].astype(F32)
            for d in range(s.ny - 1):
                share = share + q_recv[it, p, d, 0:tp].astype(F32)
            mine = v.at[it, own_q, p, pl.ds(y * tp, tp)]
            for i in range(tp):
                group = lax.rem(y * tp + i, s.groups)
                raw = share[i] * coef[0, group] - previous[p, i] * coef[1, group]
                previous[p, i] = raw
                v[it, own_q, p, y * tp + i] = raw.astype(BF16)
            for d in far_first(s.ny):
                send(mine, mine, yg_ss.at[it, p], yg_rs.at[it, p], in_y[d])

        def applied(p, q):
            return lax.dot_general(
                from_tiles(v[it, q, p, 0 : s.parts[p].tb], s.groups),
                g[q, :, s.parts[p].lanes],
                (((1,), (1,)), ((), ())),
                preferred_element_type=F32,
            )

        order = far_first(s.nx)
        for p in range(len(s.parts)):
            for d in order:
                to_mate(p, d)
        sum_start(it, left_sums())
        for p in range(len(s.parts)):
            to_mate(p, 0)
            for d in order:
                scatter_x(p, d)
            scatter_y(p)
        sum_middle(it)
        beta = sum_end(it)
        betas[it] = beta
        coef[0] = (1.0 / beta).reshape(s.groups, TILE, LANE)
        coef[1] = (beta * inverse[...]).reshape(s.groups, TILE, LANE)
        for p in range(len(s.parts)):
            spread_y(p)

        total = jnp.zeros((n, s.pixels), F32)
        for p, part in enumerate(s.parts):
            await_bytes(q_recv.at[it, p, :, 0 : part.tp], yg_rs.at[it, p])
            ready = v.at[it, own_q, p, 0 : part.tb]
            for d in far_first(s.nx):
                send(ready, ready, xg_ss.at[it, p], xg_rs.at[it, p, d - 1], in_x[d])
            send(ready, ready, cg_ss.at[it, p], cg_rs.at[it, p, 0], mate)
            total = total + applied(p, own_q)
        for p, part in enumerate(s.parts):
            for d in near_first(s.nx):
                q = from_q[0][d]
                came = v.at[it, q, p, 0 : part.tb]
                await_bytes(came, xg_rs.at[it, p, d - 1])
                send(came, came, cg_ss.at[it, p], cg_rs.at[it, p, d], mate)
                total = total + applied(p, q)
        for p, part in enumerate(s.parts):
            for d in [0] + near_first(s.nx):
                q = from_q[1][d]
                await_bytes(v.at[it, q, p, 0 : part.tb], cg_rs.at[it, p, d])
                total = total + applied(p, q)

        f_send[it, 0 : s.ft] = as_tiles(total).astype(BF16)
        if s.fz > s.ft:
            f_send[it, s.ft : s.fz] = jnp.zeros((s.fz - s.ft, TILE, LANE), BF16)
        for d in far_first(s.nz):
            piece = f_send.at[it, pl.ds(z_of[d] * s.zp, s.zp)]
            send(piece, f_recv.at[it, d - 1], z_ss.at[it], z_rs.at[it], in_z[d])
        sz_send[it] = to_row(square_sums(it))
        for d in far_first(s.nz):
            send(sz_send.at[it], sz_recv.at[it, d - 1], sz_ss.at[it], sz_rs.at[it], in_z[d])
        await_bytes(f_recv.at[it], z_rs.at[it])
        reduced = f_send[it, pl.ds(z * s.zp, s.zp)].astype(F32)
        for d in range(s.nz - 1):
            reduced = reduced + f_recv[it, d].astype(F32)
        mine = f_all.at[it, pl.ds(z * s.zp, s.zp)]
        mine[...] = reduced.astype(BF16)
        for d in far_first(s.nz):
            send(mine, mine, zg_ss.at[it], zg_rs.at[it], in_z[d])
        await_bytes(sz_recv.at[it], sz_rs.at[it])
        alpha = jnp.sqrt(from_row(sz_send[it] + jnp.sum(sz_recv[it], axis=0), n) + EPSILON)
        alphas[it] = alpha
        inverse[...] = 1.0 / alpha
        ratio = alpha / beta
        await_bytes(f_recv.at[it], zg_rs.at[it])
        for j in range(s.fb):
            lanes = slice(j * LANE, (j + 1) * LANE)
            left[:, lanes] = predicted(it, j) * inverse[...] - left[:, lanes] * ratio
        return carry

    lax.fori_loop(0, 2, iteration, 0)

    sum_start(2, left_sums())
    alpha1, alpha2, beta1, beta2 = alphas[0], alphas[1], betas[0], betas[1]
    rho1 = jnp.sqrt(alpha1 * alpha1 + beta2 * beta2)
    cosine, sine = alpha1 / rho1, beta2 / rho1
    phi1 = cosine * beta1
    phibar = sine * beta1
    theta = sine * alpha2
    rhobar = -cosine * alpha2

    first = place * (s.width // s.rows)
    block = first // LANE
    lane = lax.rem(first, LANE)
    share_width = s.width // s.rows
    cover = -(-share_width // LANE)
    shape = ((cover + 1) * LANE, cover * LANE)
    pick = lax.broadcasted_iota(jnp.int32, shape, 0) == lax.broadcasted_iota(jnp.int32, shape, 1) + lane
    pick = jnp.where(pick, 1.0, 0.0).astype(BF16)
    window = []
    for it in range(2):
        sides = []
        for k in range(cover + 1):
            b = jnp.minimum(block + k, s.width // LANE - 1)
            j = lax.rem(b, s.nb)
            p = j // s.cut
            inside = (j - p * s.cut) * s.groups
            sides.append(v[it, b // s.nb, p, pl.ds(inside, s.groups)].reshape(n, LANE))
        window.append(jnp.dot(jnp.concatenate(sides, axis=1), pick, preferred_element_type=F32))

    sum_middle(2)
    beta3 = sum_end(2)
    rho2 = jnp.sqrt(rhobar * rhobar + beta3 * beta3)
    phi2 = rhobar / rho2 * phibar
    on2 = phi2 / rho2
    weight1 = (phi1 / rho1 - on2 * (theta / rho1)) / alpha1
    weight2 = on2 / alpha2
    result = [weight1 * a + weight2 * b for a, b in zip(lane_blocks(window[0]), lane_blocks(window[1]), strict=True)]
    slip[...] = jnp.concatenate(result, axis=1)[:, 0:share_width]
    for j in range(s.fb):
        lanes = slice(j * LANE, (j + 1) * LANE)
        misfit[:, lanes] = misfit[:, lanes] - weight1 * predicted(0, j) - weight2 * predicted(1, j)

    await_bytes(halo, halo_ss.at[0])

    def settle(it, carry):
        for p, part in enumerate(s.parts):
            four = pc_send.at[it, p, :, 0 : part.tb]
            three = px_send.at[it, p, :, 0 : part.tb]
            pieces = q_recv.at[it, p, :, 0 : part.tp]
            await_bytes(four, c_ss.at[it, p])
            await_bytes(three, x_ss.at[it, p])
            await_bytes(pieces, y_ss.at[it, p])
            await_bytes(pieces, yg_ss.at[it, p])
            await_bytes(three, xg_ss.at[it, p])
            await_bytes(four, cg_ss.at[it, p])
        await_bytes(f_recv.at[it], z_ss.at[it])
        await_bytes(f_recv.at[it], zg_ss.at[it])
        await_bytes(sz_recv.at[it], sz_ss.at[it])
        return carry

    lax.fori_loop(0, 2, settle, 0)
    for i in range(3):
        await_bytes(sa_recv.at[i], sa_ss.at[i])
        await_bytes(sb_recv.at[i], sb_ss.at[i])


def body(dims, nz, data, source, near_tiles, near_rows, near_cols, near_count, far_left, far_right):
    realiz, pixels = data.shape
    rank, width = far_right.shape
    slots, tile_rows, tile_cols = near_tiles.shape
    s = Sizes(dims, nz, realiz, pixels, width, slots, rank, tile_rows, tile_cols)
    vmem = pl.BlockSpec(memory_space=pltpu.VMEM)
    pin = functools.partial(pltpu.with_memory_space_constraint, memory_space=pltpu.HBM)
    return pl.pallas_call(
        functools.partial(kernel, s),
        out_shape=(pltpu.VMEM((realiz, width // s.rows), F32), pltpu.VMEM((realiz, pixels), F32)),
        in_specs=[pl.BlockSpec(memory_space=pl.ANY)] * 8,
        out_specs=(vmem, vmem),
        scratch_shapes=scratch_shapes(s),
        compiler_params=pltpu.CompilerParams(
            collective_id=0, has_side_effects=True, vmem_limit_bytes=48 * 1024 * 1024
        ),
    )(
        pin(data),
        pin(source.reshape(1, pixels)),
        pin(near_rows.reshape(slots)),
        pin(near_cols.reshape(slots)),
        near_count,
        pin(near_tiles),
        pin(far_left),
        pin(far_right),
    )


def solution(mesh, dims=(4, 8, 2)):
    return jax.shard_map(
        functools.partial(body, dims, mesh.shape["cols"]),
        mesh=mesh,
        in_specs=(
            P(None, "rows"),
            P("rows"),
            P("rows", "cols", None),
            P("rows", "cols"),
            P("rows", "cols"),
            P("rows", "cols"),
            P("cols", "rows"),
            P("rows", "cols"),
        ),
        out_specs=(P(None, ("cols", "rows")), P(None, "rows")),
        check_vma=False,
    )
```
